256 devices in a mesh: img: 64 (over y, x_lo, z), ori: 4 (over x_hi, core).
Axes of the slice: x: 4 (x_hi: 2, x_lo: 2; x = x_hi * 2 + x_lo), y: 4, z: 8, core: 2. Of those that a mesh axis runs over, the one named last changes fastest.
Arguments:
- images: bfloat16 [65536, 4096], P('img'), may hold values from -34 to 34
- img_scale: float32 [65536], P('img'), may hold values from 0.5 to 2
- references: bfloat16 [2048, 4096], P('ori', 'img'), may hold values from -4 to 4
- pattern: int32 [65536, 8], P('img', 'ori'), may hold values from 0 to 1, as said below
- tile_owner: int32 [4, 16384, 1], P('ori', 'img'), may hold values from 0 to 63; in each aligned block of 256 rows (0 to 255, 256 to 511, ..., all dimensions but the last counted through in order) at most 12 rows name the same one
- tile_brick: int32 [4, 16384], P('ori', 'img'), may hold values from 0 to 15
- tile_block: int32 [4, 16384], P('ori', 'img'), may hold values from 0 to 7
- distance_weights: bfloat16 [8, 128, 512], replicated, may hold values from -0.0625 to 0.0625
Outputs:
- bricks: float32 [1024, 512], P(('img', 'ori'))
- log_evidence: float32 [65536], P('img')
The draws below stay inside these ranges and needn't reach their ends.
Inputs may be any that keep to these rules, and one draw needn't show every extreme that they name: `pattern`: each image has at least one orientation group set. `tile_owner`: among the 256 tiles of each aligned block, at most 12 name the same owner, and some block reaches 12.
All inputs are finite; a program needn't handle non-finite values.
Results may differ from the reference program's by a relative error of at most 0.002.
Values may be sent and summed in bfloat16 or wider, within the bound.
No kernel may reach another device: no remote copies, remote signals or barrier semaphores. Data moves between devices by JAX's collectives and lax.ppermute only.
A program may use at most 128 MiB of HBM per device.

```python
import math
import jax
import jax.numpy as jnp
import numpy as np
from jax import lax

F = 4096
TS = 128
GROUP = 256
NGROUP = 8
VOX = 512
NPOS = 8
IMG_DEV = 1024
BRICK_DEV = 16
NIMG = 65536
NREF = 2048
TPR = 32
TILES_ORI = 16384
TILES_DEV = 256
CAP = 12
NBRICK = 1024
FAN = 8192
N_IMG = 64
N_ORI = 4


def shared_refs(key):
    return jax.random.truncated_normal(jax.random.fold_in(key, 11), -4.0, 4.0, (NREF, F), jnp.float32)


def forced_group(key):
    return jax.random.randint(jax.random.fold_in(key, 12), (NIMG,), 0, NGROUP)


def draw_references(key, part):
    return shared_refs(key).astype(jnp.bfloat16)


def draw_pattern(key, part):
    coin_flips = jax.random.randint(jax.random.fold_in(key, 15), (NIMG, NGROUP), 0, 2)
    forced = (jnp.arange(NGROUP)[None, :] == forced_group(key)[:, None]).astype(jnp.int32)
    return jnp.maximum(coin_flips, forced)


def draw_images(key, part):
    noise_field = jax.random.truncated_normal(jax.random.fold_in(key, 13), -5.0, 5.0, (NIMG, F), jnp.float32)
    return noise_field.astype(jnp.bfloat16)


def place_ends(drawn, stream_key, smallest, top_value):
    extent = drawn.shape
    place = [jax.random.randint(jax.random.fold_in(stream_key, axis), (), 0, extent[axis]) for axis in range(len(extent))]
    drawn = drawn.at[tuple(place)].set(smallest)
    longest = extent.index(max(extent))
    place[longest] = (place[longest] + 1) % extent[longest]
    return drawn.at[tuple(place)].set(top_value)


def steps_of(stream_key, extent, cuts, least, high):
    factor_of = 1.0
    for axis_at, blocks in cuts:
        steps = jax.random.uniform(jax.random.fold_in(jax.random.fold_in(stream_key, 6), axis_at), (blocks,), jnp.float32, least / len(cuts), high / len(cuts))
        factor_of = factor_of * jnp.repeat(jnp.exp(steps), extent[axis_at] // blocks).reshape((-1,) + (1,) * (len(extent) - 1 - axis_at))
    return factor_of


def deal_out(key, own, number, rows, number_of, top, bound, lean):
    sequence = jax.random.permutation(key, number_of)
    heavy_load, ordinary = load_shares(number_of, rows * top, bound, lean, True), load_shares(number_of, rows * top, bound, lean, False)
    places = jnp.arange(number_of)

    def named(sizes, turn):
        used = int((sizes > 0).sum())
        fixed = max(1, used // 4)
        passed = fixed + (places - fixed + turn * (used - fixed)) % max(1, number_of - fixed)
        return jnp.zeros((number_of,), jnp.int32).at[sequence[jnp.where(places < fixed, places, passed)]].set(jnp.asarray(sizes, jnp.int32))

    sizes = jnp.where(number % 4 == 0, named(heavy_load, number // 4), named(ordinary, number - number // 4 - 1))
    mixed = jax.random.permutation(jax.random.fold_in(own, 3), number_of)
    giver, receiver = mixed[0:number_of // 2 * 2:2], mixed[1:number_of // 2 * 2:2]
    room = jnp.minimum(sizes[giver] - 1, bound - sizes[receiver]) // 2
    room = jnp.where((giver == sequence[0]) | (receiver == sequence[0]) | (sizes[receiver] == 0), 0, jnp.maximum(room, 0))
    passed = jax.random.randint(jax.random.fold_in(own, 4), (number_of // 2,), 0, 1 << 20) % (room + 1)
    sizes = sizes.at[giver].add(-passed).at[receiver].add(passed)
    members = jnp.searchsorted(jnp.cumsum(sizes), jnp.arange(rows * top), side="right").astype(jnp.int32)
    grid = members.reshape(top, rows).T
    grid = grid[jax.random.permutation(jax.random.fold_in(own, 1), rows)]
    turn = jax.random.randint(jax.random.fold_in(own, 2), (rows, 1), 0, top)
    return jnp.take_along_axis(grid, (jnp.arange(top)[None, :] + turn) % top, axis=1)


def load_shares(count, total, bound, skew, full):
    weights = [(1 << 20) // math.isqrt(grade ** skew) + 1 for grade in range(1, count + 1)]
    largest = bound if full else min(bound, max(-(-total // count), total * weights[0] // sum(weights)))
    least = 1 if total - largest >= count - 1 else 0
    counts, rest = [largest] + [least] * (count - 1), total - largest - least * (count - 1)
    while rest > 0:
        free = [i for i in range(1, count) if counts[i] < largest] or [i for i in range(1, count) if counts[i] < bound]
        whole, left = sum([weights[i] for i in free]), rest
        for i in free:
            more = min(bound - counts[i], max(1, left * weights[i] // whole), rest)
            counts[i] = counts[i] + more
            rest = rest - more
    return np.array(counts)


def normal_values(own_key, dims, spread, bound, kind=jnp.bfloat16):
    return jnp.clip(spread * jax.random.normal(own_key, dims, jnp.float32), -bound, bound).astype(kind)


def setup_inputs(seed: int = 0) -> dict:
    arg_keys = jax.random.split(jax.random.key(seed), 9)
    images = draw_images(jax.random.fold_in(arg_keys[8], 71), 0)
    img_scale = jnp.clip(jnp.exp(math.log(2.0) - 1.3862944 * jax.random.uniform(arg_keys[1], (NIMG,), jnp.float32) ** steps_of(arg_keys[1], (NIMG,), ((0, 64),), -0.2, 0.2)), 0.5, 2.0)
    references = draw_references(jax.random.fold_in(arg_keys[8], 71), 0)
    pattern = draw_pattern(jax.random.fold_in(arg_keys[8], 71), 0)
    tile_owner_keys = jax.random.split(jax.random.fold_in(arg_keys[4], 1), N_ORI * TILES_ORI // TILES_DEV)
    tile_owner_turns = jax.random.permutation(jax.random.fold_in(arg_keys[4], 3), N_ORI * TILES_ORI // TILES_DEV)
    tile_owner = jax.vmap(lambda own, number: deal_out(jax.random.fold_in(arg_keys[4], 2), own, number, TILES_DEV, N_IMG, 1, CAP, 2))(tile_owner_keys, tile_owner_turns).reshape((N_ORI, TILES_ORI, 1))
    tile_brick = place_ends(jax.random.randint(arg_keys[5], (N_ORI, TILES_ORI), 0, BRICK_DEV), jax.random.fold_in(arg_keys[5], 1), 0, BRICK_DEV - 1).astype(jnp.int32)
    tile_block = place_ends(jax.random.randint(arg_keys[6], (N_ORI, TILES_ORI), 0, NPOS), jax.random.fold_in(arg_keys[6], 1), 0, NPOS - 1).astype(jnp.int32)
    distance_weights = normal_values(arg_keys[7], (NPOS, TS, VOX), FAN ** -0.5, 0.0625)
    return {"images": images, "img_scale": img_scale, "references": references, "pattern": pattern, "tile_owner": tile_owner, "tile_brick": tile_brick, "tile_block": tile_block, "distance_weights": distance_weights}


def reference(images, img_scale, references, pattern, tile_owner, tile_brick, tile_block, distance_weights):
    inv_root = 1.0 / math.sqrt(F)
    image_blocks = images.reshape(NIMG // IMG_DEV, IMG_DEV, F)
    scale_blocks = img_scale.reshape(NIMG // IMG_DEV, IMG_DEV)
    flag_blocks = pattern.reshape(NIMG // IMG_DEV, IMG_DEV, NGROUP)

    def visit(totals, block):
        pixels, scales, flags = block
        raw_scores = jnp.dot(pixels, references.T, preferred_element_type=jnp.float32)
        scores = raw_scores * scales[:, None] * inv_root
        active = jnp.repeat(flags > 0, GROUP, axis=1)
        masked = jnp.where(active, scores, -1e+30)
        peak = lax.optimization_barrier(jnp.max(masked, axis=1))
        expo = jnp.where(active, jnp.exp(masked - peak[:, None]), 0.0)
        mass = lax.optimization_barrier(jnp.sum(expo, axis=1))
        weights = expo / mass[:, None]
        scaled = (weights * scales[:, None]).astype(jnp.bfloat16)
        totals = totals + jnp.dot(scaled.T, pixels, preferred_element_type=jnp.float32)
        return (totals, peak + jnp.log(mass))
    start_sums = jnp.zeros((NREF, F), jnp.float32)
    class_sums, evidence = lax.scan(visit, start_sums, (image_blocks, scale_blocks, flag_blocks))
    log_evidence = evidence.reshape(NIMG)
    tiles = class_sums.reshape(NREF * TPR, TS)
    tile_code = ((tile_owner.reshape(-1) * BRICK_DEV + tile_brick.reshape(-1)) * NPOS + tile_block.reshape(-1)).astype(jnp.int32)
    collected = jax.ops.segment_sum(tiles, tile_code, num_segments=NBRICK * NPOS)
    bricks = jnp.einsum('bpt,ptv->bv', collected.reshape(NBRICK, NPOS, TS), distance_weights.astype(jnp.float32), precision=lax.Precision.HIGHEST)
    return (bricks, log_evidence)
```

```python
import functools
import math

import jax
import jax.numpy as jnp
from jax import lax
from jax.experimental import pallas as pl
from jax.experimental.pallas import tpu as pltpu
from jax.sharding import Mesh
from jax.sharding import PartitionSpec as P

BF16, F32, I32 = jnp.bfloat16, jnp.float32, jnp.int32
AXES = {"y": 4, "xl": 2, "z": 8, "xh": 2, "core": 2}
IMG, ORI = ("y", "xl", "z"), ("xh", "core")
REFS, VALUES, IMAGES = 512, 4096, 1024
SHARE = 64
CELLS = 8192
LANES = 128
VMEM = 58 * 2**20


def moved(x, axes, target):
    sizes = [AXES[a] for a in axes]
    pairs = []
    for i in range(math.prod(sizes)):
        at, k = [], i
        for n in reversed(sizes):
            at.insert(0, k % n)
            k //= n
        to = 0
        for n, c in zip(sizes, target(*at)):
            to = to * n + c % n
        pairs.append((i, to))
    return lax.ppermute(x, axes, pairs)


def along_x(x, step):
    def target(xl, xh):
        at = (xh * 2 + xl + step) % 4
        return at % 2, at // 2

    return moved(x, ("xl", "xh"), target)


def spread(x, axes):
    n = math.prod(AXES[a] for a in axes)
    return lax.all_to_all(jnp.broadcast_to(x[None], (n, *x.shape)), axes, 0, 0)


def gathered_references(references, cut):
    share = references.T
    near = spread(share[:cut], ("y", "xl"))
    ended_z = lax.all_gather(near, "z", axis=0)
    own = spread(share[cut:], ("z",))
    other = moved(own, ("xl",), lambda xl: (xl + 1,))
    pair = jnp.stack([own, other])
    ended_y = [pair] + [moved(pair, ("y",), lambda y: (y + d,)) for d in (1, 2, 3)]
    return [ended_z, *ended_y]


def eye():
    return lax.broadcasted_iota(I32, (LANES, LANES), 0) == lax.broadcasted_iota(
        I32, (LANES, LANES), 1
    )


def scores_kernel(
    cut, me, images, scale, pattern, by_z, y0, y1, y2, y3, expo, peaks, masses, refs, sems
):
    step = pl.program_id(0)
    rows = images.shape[0]

    @pl.when(step == 0)
    def _():
        copies = [(by_z.at[z], refs.at[:, z, pl.ds(0, cut)]) for z in range(8)]
        for d, part in enumerate((y0, y1, y2, y3)):
            y = (me[0] + 4 - d) % 4
            for r in range(2):
                xl = (me[1] + r) % 2
                copies.append((part.at[r], refs.at[y * 2 + xl, :, pl.ds(cut, SHARE - cut)]))
        copies = [pltpu.make_async_copy(a, b, sems.at[i]) for i, (a, b) in enumerate(copies)]
        for c in copies:
            c.start()
        for c in copies:
            c.wait()

    total = jnp.zeros((rows, REFS), F32)
    wide = 8 * SHARE
    for q in range(8):
        total += jnp.dot(
            images[:, q * wide : (q + 1) * wide],
            refs[q].reshape(wide, REFS),
            preferred_element_type=F32,
        )
    scores = total * scale[...] * (1.0 / math.sqrt(VALUES))
    group = lax.broadcasted_iota(I32, (rows, REFS), 1) // (REFS // 2)
    flags = pattern[...]
    active = jnp.where(group == 0, flags[:, 0:1], flags[:, 1:2]) > 0
    masked = jnp.where(active, scores, -1e30)
    peak = jnp.max(masked, axis=1, keepdims=True)
    value = jnp.where(active, jnp.exp(masked - peak), 0.0)
    mass = jnp.sum(value, axis=1, keepdims=True)
    expo[...] = value
    for j in range(rows // LANES):
        part = slice(j * LANES, (j + 1) * LANES)
        row = pl.ds(step * (rows // LANES) + j, 1)
        peaks[row, :] = jnp.sum(jnp.where(eye(), peak[part], 0.0), axis=0, keepdims=True)
        masses[row, :] = jnp.sum(jnp.where(eye(), mass[part], 0.0), axis=0, keepdims=True)


def scores_of(me, images, scale, pattern, parts, cut, rows=256):
    here = pl.BlockSpec((8, LANES), lambda i: (0, 0))
    return pl.pallas_call(
        functools.partial(scores_kernel, cut),
        grid=(IMAGES // rows,),
        in_specs=[
            pl.BlockSpec(memory_space=pltpu.SMEM),
            pl.BlockSpec((rows, VALUES), lambda i: (i, 0)),
            pl.BlockSpec((rows, 1), lambda i: (i, 0)),
            pl.BlockSpec((rows, 2), lambda i: (i, 0)),
        ]
        + [pl.BlockSpec(memory_space=pl.ANY)] * len(parts),
        out_specs=[pl.BlockSpec((rows, REFS), lambda i: (i, 0)), here, here],
        out_shape=[
            jax.ShapeDtypeStruct((IMAGES, REFS), F32),
            jax.ShapeDtypeStruct((8, LANES), F32),
            jax.ShapeDtypeStruct((8, LANES), F32),
        ],
        scratch_shapes=[
            pltpu.VMEM((8, 8, SHARE, REFS), BF16),
            pltpu.SemaphoreType.DMA((16,)),
        ],
        compiler_params=pltpu.CompilerParams(vmem_limit_bytes=VMEM),
        name="scores",
    )(me, images, scale, pattern, *parts)


UNROLL = 32


def bricks_kernel(cells, factor, expo, images, weights, out, scaled, tiles, c0, c1, c2, c3):
    step = pl.program_id(0)
    sums = (c0, c1, c2, c3)

    @pl.when(step == 0)
    def _():
        for j in range(IMAGES // LANES):
            part = slice(j * LANES, (j + 1) * LANES)
            column = jnp.sum(
                jnp.where(eye(), factor[j : j + 1, :], 0.0), axis=1, keepdims=True
            )
            scaled[:, part] = (expo[part, :] * column).T.astype(BF16)

        def clear(i, _):
            for c in sums:
                c[pl.ds(i * 256, 256), :] = jnp.zeros((256, LANES), F32)
            return 0

        lax.fori_loop(0, CELLS // 256, clear, 0)

    block = jnp.dot(scaled[...], images[...], preferred_element_type=F32)
    tiles[0:REFS, :] = block[:, 0:LANES]
    tiles[REFS:, :] = block[:, LANES:]

    def add(i, _):
        for u in range(UNROLL):
            row = i * UNROLL + u
            cell = pl.ds(cells[step * (2 * REFS) + row], 1)
            c = sums[u % 4]
            c[cell, :] = c[cell, :] + tiles[pl.ds(row, 1), :]
        return 0

    lax.fori_loop(0, 2 * REFS // UNROLL, add, 0)

    @pl.when(step == pl.num_programs(0) - 1)
    def _():
        for r in range(0, 1024, 256):
            total = jnp.zeros((256, weights.shape[2]), F32)
            for p in range(8):
                part = pl.ds(p * 1024 + r, 256)
                cell = (c0[part, :] + c1[part, :]) + (c2[part, :] + c3[part, :])
                high = cell.astype(BF16)
                low = (cell - high.astype(F32)).astype(BF16)
                w = weights[p]
                total += jnp.dot(
                    jnp.concatenate([high, low], axis=1),
                    jnp.concatenate([w, w], axis=0),
                    preferred_element_type=F32,
                )
            out[r : r + 256, :] = total


def bricks_of(cells, factor, expo, images, weights):
    positions, width, voxels = weights.shape
    wide = 2 * LANES
    return pl.pallas_call(
        bricks_kernel,
        grid=(VALUES // wide,),
        in_specs=[
            pl.BlockSpec(memory_space=pltpu.SMEM),
            pl.BlockSpec((8, LANES), lambda i: (0, 0)),
            pl.BlockSpec((IMAGES, REFS), lambda i: (0, 0)),
            pl.BlockSpec((IMAGES, wide), lambda i: (0, i)),
            pl.BlockSpec((positions, width, voxels), lambda i: (0, 0, 0)),
        ],
        out_specs=pl.BlockSpec((CELLS // positions, voxels), lambda i: (0, 0)),
        out_shape=jax.ShapeDtypeStruct((CELLS // positions, voxels), F32),
        scratch_shapes=[
            pltpu.VMEM((REFS, IMAGES), BF16),
            pltpu.VMEM((2 * REFS, LANES), F32),
        ]
        + [pltpu.VMEM((CELLS, LANES), F32)] * 4,
        compiler_params=pltpu.CompilerParams(vmem_limit_bytes=VMEM),
        name="bricks",
    )(cells, factor, expo, images, weights)


def merged(pairs):
    peak = functools.reduce(jnp.maximum, [p for p, _ in pairs])
    return peak, sum(m * jnp.exp(p - peak) for p, m in pairs)


def brick_share(terms, me_free=None):
    voxels = terms.shape[1]
    x = terms.reshape(2, -1, voxels)
    x = x[0] + moved(x[1], ("core",), lambda c: (c + 1,))
    x = x.reshape(4, -1, voxels)
    got = [moved(x[d].astype(BF16), ("y",), lambda y: (y + d,)) for d in (1, 2, 3)]
    x = x[0] + sum(g.astype(F32) for g in got)
    x = x.reshape(4, -1, voxels)
    got = [along_x(x[d], d) for d in (1, 2, 3)]
    x = x[0] + sum(got)
    x = x.reshape(8, -1, voxels)
    for half in (4, 2, 1):
        x = x[:half] + moved(x[half:], ("z",), lambda z: (z ^ half,))
    return x[0]


def body(images, img_scale, references, pattern, tile_owner, tile_brick, tile_block, weights):
    cut = 32
    at = {a: lax.axis_index(a) for a in AXES}
    parts = gathered_references(references, cut)

    code = tile_owner.reshape(-1) * 16 + tile_brick.reshape(-1)
    code = code * 8 + tile_block.reshape(-1)
    code = lax.all_gather(code, IMG, axis=0, tiled=True).reshape(REFS, -1).T.reshape(-1)
    block, row = code % 8, code // 8 % 4
    core, xh = code // 32 % 2, code // 64 % 2
    z, xl, y = code // 128 % 8, code // 1024 % 2, code // 2048
    away = jnp.bitwise_xor(core, at["core"]) * 4 + (y - at["y"]) % 4
    away = away * 4 + (xh * 2 + xl - at["xh"] * 2 - at["xl"]) % 4
    away = away * 8 + jnp.bitwise_xor(z, at["z"])
    cells = block * (CELLS // 8) + away * 4 + row

    me = jnp.stack([at["y"], at["xl"]]).astype(I32)
    expo, peak, mass = scores_of(me, images, img_scale[:, None], pattern, parts, cut)
    mine = jnp.concatenate([peak, mass])
    others = [
        moved(mine, ORI, lambda h, c: (h + dh, c + dc)) for dh, dc in ((0, 1), (1, 0), (1, 1))
    ]
    all_peak, all_mass = merged([(s[:8], s[8:]) for s in (mine, *others)])
    factor = jnp.exp(peak - all_peak) / all_mass * img_scale.reshape(8, LANES)
    terms = bricks_of(cells, factor, expo, images, weights)
    log_evidence = (all_peak + jnp.log(all_mass)).reshape(-1)
    return brick_share(terms), log_evidence


def solution(mesh):
    cut_mesh = Mesh(mesh.devices.reshape(*AXES.values()), tuple(AXES))
    placed = (
        P(IMG, None),
        P(IMG),
        P(ORI, IMG),
        P(IMG, ORI),
        P(ORI, IMG, None),
        P(ORI, IMG),
        P(ORI, IMG),
        P(),
    )
    return jax.shard_map(
        body,
        mesh=cut_mesh,
        in_specs=placed,
        out_specs=(P(IMG + ORI, None), P(IMG)),
        check_vma=False,
    )
```

```python
import functools
import math

import jax
import jax.numpy as jnp
from jax import lax
from jax.experimental import pallas as pl
from jax.experimental.pallas import tpu as pltpu
from jax.sharding import Mesh
from jax.sharding import PartitionSpec as P

BF16, F32, I32 = jnp.bfloat16, jnp.float32, jnp.int32
AXES = {"y": 4, "xl": 2, "z": 8, "xh": 2, "core": 2}
IMG, ORI = ("y", "xl", "z"), ("xh", "core")
REFS, VALUES, IMAGES = 512, 4096, 1024
SHARE = 64
CELLS = 8192
LANES = 128
VMEM = 58 * 2**20


def moved(x, axes, target):
    sizes = [AXES[a] for a in axes]
    pairs = []
    for i in range(math.prod(sizes)):
        at, k = [], i
        for n in reversed(sizes):
            at.insert(0, k % n)
            k //= n
        to = 0
        for n, c in zip(sizes, target(*at)):
            to = to * n + c % n
        pairs.append((i, to))
    return lax.ppermute(x, axes, pairs)


def along_x(x, step):
    def target(xl, xh):
        at = (xh * 2 + xl + step) % 4
        return at % 2, at // 2

    return moved(x, ("xl", "xh"), target)


def spread(x, axes):
    n = math.prod(AXES[a] for a in axes)
    return lax.all_to_all(jnp.broadcast_to(x[None], (n, *x.shape)), axes, 0, 0)


def gathered_references(references, codes, cut):
    share = references.T
    more = jnp.pad(codes.astype(BF16)[None], ((0, 7), (0, 0)))
    near = spread(jnp.concatenate([share[:cut], more]), ("y", "xl"))
    ended_z = lax.all_gather(near, "z", axis=0)
    own = spread(share[cut:], ("z",))
    other = moved(own, ("xl",), lambda xl: (xl + 1,))
    pair = jnp.stack([own, other])
    ended_y = [pair] + [moved(pair, ("y",), lambda y: (y + d,)) for d in (1, 2, 3)]
    return [ended_z, *ended_y]


def eye():
    return lax.broadcasted_iota(I32, (LANES, LANES), 0) == lax.broadcasted_iota(
        I32, (LANES, LANES), 1
    )


def scores_kernel(
    cut, me, images, scale, pattern, by_z, y0, y1, y2, y3, expo, stats, refs, sems
):
    step = pl.program_id(0)
    rows = images.shape[0]

    @pl.when(step == 0)
    def _():
        copies = [(by_z.at[z, :, pl.ds(0, cut)], refs.at[:, z, pl.ds(0, cut)]) for z in range(8)]
        for d, part in enumerate((y0, y1, y2, y3)):
            y = (me[0] + 4 - d) % 4
            for r in range(2):
                xl = (me[1] + r) % 2
                copies.append((part.at[r], refs.at[y * 2 + xl, :, pl.ds(cut, SHARE - cut)]))
        copies = [pltpu.make_async_copy(a, b, sems.at[i]) for i, (a, b) in enumerate(copies)]
        for c in copies:
            c.start()
        for c in copies:
            c.wait()

    total = jnp.zeros((rows, REFS), F32)
    wide = 8 * SHARE
    for q in range(8):
        total += jnp.dot(
            images[:, q * wide : (q + 1) * wide],
            refs[q].reshape(wide, REFS),
            preferred_element_type=F32,
        )
    scores = total * scale[...] * (1.0 / math.sqrt(VALUES))
    group = lax.broadcasted_iota(I32, (rows, REFS), 1) // (REFS // 2)
    flags = pattern[...]
    active = jnp.where(group == 0, flags[:, 0:1], flags[:, 1:2]) > 0
    masked = jnp.where(active, scores, -1e30)
    peak = jnp.max(masked, axis=1, keepdims=True)
    value = jnp.where(active, jnp.exp(masked - peak), 0.0)
    mass = jnp.sum(value, axis=1, keepdims=True)
    expo[...] = value
    for j in range(rows // LANES):
        part = slice(j * LANES, (j + 1) * LANES)
        at = step * (rows // LANES) + j
        for k, column in enumerate((peak, mass)):
            stats[pl.ds(k * 8 + at, 1), :] = jnp.sum(
                jnp.where(eye(), column[part], 0.0), axis=0, keepdims=True
            )


def scores_of(me, images, scale, pattern, parts, cut, rows=256):
    return pl.pallas_call(
        functools.partial(scores_kernel, cut),
        grid=(IMAGES // rows,),
        in_specs=[
            pl.BlockSpec(memory_space=pltpu.SMEM),
            pl.BlockSpec((rows, VALUES), lambda i: (i, 0)),
            pl.BlockSpec((rows, 1), lambda i: (i, 0)),
            pl.BlockSpec((rows, 2), lambda i: (i, 0)),
        ]
        + [pl.BlockSpec(memory_space=pl.ANY)] * len(parts),
        out_specs=[
            pl.BlockSpec((rows, REFS), lambda i: (i, 0)),
            pl.BlockSpec((16, LANES), lambda i: (0, 0)),
        ],
        out_shape=[
            jax.ShapeDtypeStruct((IMAGES, REFS), F32),
            jax.ShapeDtypeStruct((16, LANES), F32),
        ],
        scratch_shapes=[
            pltpu.VMEM((8, 8, SHARE, REFS), BF16),
            pltpu.SemaphoreType.DMA((16,)),
        ],
        compiler_params=pltpu.CompilerParams(vmem_limit_bytes=VMEM),
        name="scores",
    )(me, images, scale, pattern, *parts)


UNROLL = 32


def bricks_kernel(
    cells, scale, s0, s1, s2, s3, expo, images, weights,
    keep, send, evidence, scaled, tiles, c0, c1, c2, c3,
):
    step = pl.program_id(0)
    sums = (c0, c1, c2, c3)

    @pl.when(step == 0)
    def _():
        pairs = [(s[0:8, :], s[8:16, :]) for s in (s0, s1, s2, s3)]
        peak = functools.reduce(jnp.maximum, [p for p, _ in pairs])
        mass = sum(m * jnp.exp(p - peak) for p, m in pairs)
        evidence[...] = peak + jnp.log(mass)
        factor = jnp.exp(pairs[0][0] - peak) / mass * scale[...]
        for j in range(IMAGES // LANES):
            part = slice(j * LANES, (j + 1) * LANES)
            column = jnp.sum(
                jnp.where(eye(), factor[j : j + 1, :], 0.0), axis=1, keepdims=True
            )
            scaled[:, part] = (expo[part, :] * column).T.astype(BF16)

        def clear(i, _):
            for c in sums:
                c[pl.ds(i * 256, 256), :] = jnp.zeros((256, LANES), F32)
            return 0

        lax.fori_loop(0, CELLS // 256, clear, 0)

    block = jnp.dot(scaled[...], images[...], preferred_element_type=F32)
    tiles[0:REFS, :] = block[:, 0:LANES]
    tiles[REFS:, :] = block[:, LANES:]

    def add(i, _):
        for u in range(UNROLL):
            row = i * UNROLL + u
            cell = pl.ds(cells[step * (2 * REFS) + row], 1)
            c = sums[u % 4]
            c[cell, :] = c[cell, :] + tiles[pl.ds(row, 1), :]
        return 0

    lax.fori_loop(0, 2 * REFS // UNROLL, add, 0)

    @pl.when(step == pl.num_programs(0) - 1)
    def _():
        for r in range(0, 1024, 256):
            total = jnp.zeros((256, weights.shape[2]), F32)
            for p in range(8):
                part = pl.ds(p * 1024 + r, 256)
                cell = (c0[part, :] + c1[part, :]) + (c2[part, :] + c3[part, :])
                high = cell.astype(BF16)
                low = (cell - high.astype(F32)).astype(BF16)
                w = weights[p]
                total += jnp.dot(
                    jnp.concatenate([high, low], axis=1),
                    jnp.concatenate([w, w], axis=0),
                    preferred_element_type=F32,
                )
            if r < 512:
                keep[r : r + 256, :] = total
            else:
                send[r - 512 : r - 256, :] = total


def bricks_of(cells, scale, stats, expo, images, weights):
    positions, width, voxels = weights.shape
    wide = 2 * LANES
    half = pl.BlockSpec((512, voxels), lambda i: (0, 0))
    return pl.pallas_call(
        bricks_kernel,
        grid=(VALUES // wide,),
        in_specs=[
            pl.BlockSpec(memory_space=pltpu.SMEM),
            pl.BlockSpec((8, LANES), lambda i: (0, 0)),
            *[pl.BlockSpec((16, LANES), lambda i: (0, 0))] * 4,
            pl.BlockSpec((IMAGES, REFS), lambda i: (0, 0)),
            pl.BlockSpec((IMAGES, wide), lambda i: (0, i)),
            pl.BlockSpec((positions, width, voxels), lambda i: (0, 0, 0)),
        ],
        out_specs=[half, half, pl.BlockSpec((8, LANES), lambda i: (0, 0))],
        out_shape=[
            jax.ShapeDtypeStruct((512, voxels), F32),
            jax.ShapeDtypeStruct((512, voxels), F32),
            jax.ShapeDtypeStruct((8, LANES), F32),
        ],
        scratch_shapes=[
            pltpu.VMEM((REFS, IMAGES), BF16),
            pltpu.VMEM((2 * REFS, LANES), F32),
        ]
        + [pltpu.VMEM((CELLS, LANES), F32)] * 4,
        compiler_params=pltpu.CompilerParams(vmem_limit_bytes=VMEM),
        name="bricks",
    )(cells, scale, *stats, expo, images, weights)


def brick_share(keep, send):
    voxels = keep.shape[1]
    x = keep + moved(send, ("core",), lambda c: (c + 1,))
    x = x.reshape(4, -1, voxels)
    got = [moved(x[d].astype(BF16), ("y",), lambda y: (y + d,)) for d in (1, 2, 3)]
    x = x[0] + sum(g.astype(F32) for g in got)
    x = x.reshape(4, -1, voxels)
    got = [along_x(x[d], d) for d in (1, 2, 3)]
    x = x[0] + sum(got)
    x = x.reshape(8, -1, voxels)
    for half in (4, 2, 1):
        x = x[:half] + moved(x[half:], ("z",), lambda z: (z ^ half,))
    return x[0]


def body(images, img_scale, references, pattern, tile_owner, tile_brick, tile_block, weights):
    cut = 32
    at = {a: lax.axis_index(a) for a in AXES}
    owned = tile_owner.reshape(-1)
    codes = jnp.concatenate([owned, (tile_brick * 8 + tile_block).reshape(-1)])
    parts = gathered_references(references, codes, cut)

    code = parts[0][:, :, cut].astype(I32)
    code = code[..., : owned.size] * 128 + code[..., owned.size :]
    code = code.swapaxes(0, 1).reshape(REFS, -1).T.reshape(-1)
    block, row = code % 8, code // 8 % 4
    core, xh = code // 32 % 2, code // 64 % 2
    z, xl, y = code // 128 % 8, code // 1024 % 2, code // 2048
    away = jnp.bitwise_xor(core, at["core"]) * 4 + (y - at["y"]) % 4
    away = away * 4 + (xh * 2 + xl - at["xh"] * 2 - at["xl"]) % 4
    away = away * 8 + jnp.bitwise_xor(z, at["z"])
    cells = block * (CELLS // 8) + away * 4 + row

    me = jnp.stack([at["y"], at["xl"]]).astype(I32)
    expo, stats = scores_of(me, images, img_scale[:, None], pattern, parts, cut)
    others = [
        moved(stats, ORI, lambda h, c: (h + dh, c + dc)) for dh, dc in ((0, 1), (1, 0), (1, 1))
    ]
    scale = img_scale.reshape(8, LANES)
    keep, send, evidence = bricks_of(cells, scale, (stats, *others), expo, images, weights)
    return brick_share(keep, send), evidence.reshape(-1)


def solution(mesh):
    cut_mesh = Mesh(mesh.devices.reshape(*AXES.values()), tuple(AXES))
    placed = (
        P(IMG, None),
        P(IMG),
        P(ORI, IMG),
        P(IMG, ORI),
        P(ORI, IMG, None),
        P(ORI, IMG),
        P(ORI, IMG),
        P(),
    )
    return jax.shard_map(
        body,
        mesh=cut_mesh,
        in_specs=placed,
        out_specs=(P(IMG + ORI, None), P(IMG)),
        check_vma=False,
    )
```

```python
import functools
import math

import jax
import jax.numpy as jnp
from jax import lax
from jax.experimental import pallas as pl
from jax.experimental.pallas import tpu as pltpu
from jax.sharding import Mesh
from jax.sharding import PartitionSpec as P

BF16, F32, I32 = jnp.bfloat16, jnp.float32, jnp.int32
AXES = {"y": 4, "xl": 2, "z": 8, "xh": 2, "core": 2}
IMG, ORI = ("y", "xl", "z"), ("xh", "core")
REFS, VALUES, IMAGES = 512, 4096, 1024
SHARE = 64
CELLS = 8192
LANES = 128
VMEM = 58 * 2**20


def moved(x, axes, target):
    sizes = [AXES[a] for a in axes]
    pairs = []
    for i in range(math.prod(sizes)):
        at, k = [], i
        for n in reversed(sizes):
            at.insert(0, k % n)
            k //= n
        to = 0
        for n, c in zip(sizes, target(*at)):
            to = to * n + c % n
        pairs.append((i, to))
    return lax.ppermute(x, axes, pairs)


def spread(x, axes):
    n = math.prod(AXES[a] for a in axes)
    return lax.all_to_all(jnp.broadcast_to(x[None], (n, *x.shape)), axes, 0, 0)


def gathered_references(references, codes, cut):
    share = references.T
    more = jnp.pad(codes.astype(BF16)[None], ((0, 7), (0, 0)))
    near = spread(jnp.concatenate([share[:cut], more]), ("y", "xl"))
    ended_z = lax.all_gather(near, "z", axis=0)
    own = spread(share[cut:], ("z",))
    other = moved(own, ("xl",), lambda xl: (xl + 1,))
    ended_y = []
    for part in (own, other):
        ended_y.append(part)
        ended_y += [moved(part, ("y",), lambda y: (y + d,)) for d in (1, 2, 3)]
    return [ended_z, *ended_y]


def eye():
    return lax.broadcasted_iota(I32, (LANES, LANES), 0) == lax.broadcasted_iota(
        I32, (LANES, LANES), 1
    )


def scores_kernel(
    cut, me, images, scale, pattern, by_z, a0, a1, a2, a3, b0, b1, b2, b3, expo, stats, refs, sems
):
    step = pl.program_id(0)
    rows = images.shape[0]

    @pl.when(step == 0)
    def _():
        copies = [(by_z.at[z, :, pl.ds(0, cut)], refs.at[:, z, pl.ds(0, cut)]) for z in range(8)]
        for i, part in enumerate((a0, a1, a2, a3, b0, b1, b2, b3)):
            y, xl = (me[0] + 4 - i % 4) % 4, (me[1] + i // 4) % 2
            copies.append((part, refs.at[y * 2 + xl, :, pl.ds(cut, SHARE - cut)]))
        copies = [pltpu.make_async_copy(a, b, sems.at[i]) for i, (a, b) in enumerate(copies)]
        for c in copies:
            c.start()
        for c in copies:
            c.wait()

    total = jnp.zeros((rows, REFS), F32)
    wide = 8 * SHARE
    for q in range(8):
        total += jnp.dot(
            images[:, q * wide : (q + 1) * wide],
            refs[q].reshape(wide, REFS),
            preferred_element_type=F32,
        )
    scores = total * scale[...] * (1.0 / math.sqrt(VALUES))
    group = lax.broadcasted_iota(I32, (rows, REFS), 1) // (REFS // 2)
    flags = pattern[...]
    active = jnp.where(group == 0, flags[:, 0:1], flags[:, 1:2]) > 0
    masked = jnp.where(active, scores, -1e30)
    peak = jnp.max(masked, axis=1, keepdims=True)
    value = jnp.where(active, jnp.exp(masked - peak), 0.0)
    mass = jnp.sum(value, axis=1, keepdims=True)
    expo[...] = value.T
    for j in range(rows // LANES):
        part = slice(j * LANES, (j + 1) * LANES)
        at = step * (rows // LANES) + j
        for k, column in enumerate((peak, mass)):
            stats[pl.ds(k * 8 + at, 1), :] = jnp.sum(
                jnp.where(eye(), column[part], 0.0), axis=0, keepdims=True
            )


def scores_of(me, images, scale, pattern, parts, cut, rows=256):
    return pl.pallas_call(
        functools.partial(scores_kernel, cut),
        grid=(IMAGES // rows,),
        in_specs=[
            pl.BlockSpec(memory_space=pltpu.SMEM),
            pl.BlockSpec((rows, VALUES), lambda i: (i, 0)),
            pl.BlockSpec((rows, 1), lambda i: (i, 0)),
            pl.BlockSpec((rows, 2), lambda i: (i, 0)),
        ]
        + [pl.BlockSpec(memory_space=pl.ANY)] * len(parts),
        out_specs=[
            pl.BlockSpec((REFS, rows), lambda i: (0, i)),
            pl.BlockSpec((16, LANES), lambda i: (0, 0)),
        ],
        out_shape=[
            jax.ShapeDtypeStruct((REFS, IMAGES), F32),
            jax.ShapeDtypeStruct((16, LANES), F32),
        ],
        scratch_shapes=[
            pltpu.VMEM((8, 8, SHARE, REFS), BF16),
            pltpu.SemaphoreType.DMA((16,)),
        ],
        compiler_params=pltpu.CompilerParams(vmem_limit_bytes=VMEM),
        name="scores",
    )(me, images, scale, pattern, *parts)


UNROLL = 64
SUMS = 8
WIDE = 1024


def bricks_kernel(
    cells, scale, s0, s1, s2, s3, expo, images, weights,
    keep, send, evidence, scaled, tiles, *sums,
):
    step = pl.program_id(0)

    @pl.when(step == 0)
    def _():
        pairs = [(s[0:8, :], s[8:16, :]) for s in (s0, s1, s2, s3)]
        peak = functools.reduce(jnp.maximum, [p for p, _ in pairs])
        mass = sum(m * jnp.exp(p - peak) for p, m in pairs)
        evidence[...] = peak + jnp.log(mass)
        factor = jnp.exp(pairs[0][0] - peak) / mass * scale[...]
        for j in range(IMAGES // LANES):
            part = slice(j * LANES, (j + 1) * LANES)
            scaled[:, part] = (expo[:, part] * factor[j : j + 1, :]).astype(BF16)

        def clear(i, _):
            for c in sums:
                c[pl.ds(i * 256, 256), :] = jnp.zeros((256, LANES), F32)
            return 0

        lax.fori_loop(0, CELLS // 256, clear, 0)

    for n in range(0, WIDE, 256):
        block = jnp.dot(scaled[...], images[:, n : n + 256], preferred_element_type=F32)
        for k in range(2):
            at = (n // LANES + k) * REFS
            tiles[at : at + REFS, :] = block[:, k * LANES : (k + 1) * LANES]

    count = tiles.shape[0]

    def add(i, _):
        for u in range(UNROLL):
            row = i * UNROLL + u
            cell = pl.ds(cells[step * count + row], 1)
            c = sums[u % SUMS]
            c[cell, :] = c[cell, :] + tiles[pl.ds(row, 1), :]
        return 0

    lax.fori_loop(0, count // UNROLL, add, 0)

    @pl.when(step == pl.num_programs(0) - 1)
    def _():
        for r in range(0, 1024, 256):
            total = jnp.zeros((256, weights.shape[2]), F32)
            for p in range(8):
                part = pl.ds(p * 1024 + r, 256)
                cell = functools.reduce(jnp.add, [c[part, :] for c in sums])
                high = cell.astype(BF16)
                low = (cell - high.astype(F32)).astype(BF16)
                w = weights[p]
                total += jnp.dot(
                    jnp.concatenate([high, low], axis=1),
                    jnp.concatenate([w, w], axis=0),
                    preferred_element_type=F32,
                )
            if r < 512:
                keep[r : r + 256, :] = total
            else:
                send[r - 512 : r - 256, :] = total


def bricks_of(cells, scale, stats, expo, images, weights):
    positions, width, voxels = weights.shape
    half = pl.BlockSpec((512, voxels), lambda i: (0, 0))
    return pl.pallas_call(
        bricks_kernel,
        grid=(VALUES // WIDE,),
        in_specs=[
            pl.BlockSpec(memory_space=pltpu.SMEM),
            pl.BlockSpec((8, LANES), lambda i: (0, 0)),
            *[pl.BlockSpec((16, LANES), lambda i: (0, 0))] * 4,
            pl.BlockSpec((REFS, IMAGES), lambda i: (0, 0)),
            pl.BlockSpec((IMAGES, WIDE), lambda i: (0, i)),
            pl.BlockSpec((positions, width, voxels), lambda i: (0, 0, 0)),
        ],
        out_specs=[half, half, pl.BlockSpec((8, LANES), lambda i: (0, 0))],
        out_shape=[
            jax.ShapeDtypeStruct((512, voxels), F32),
            jax.ShapeDtypeStruct((512, voxels), F32),
            jax.ShapeDtypeStruct((8, LANES), F32),
        ],
        scratch_shapes=[
            pltpu.VMEM((REFS, IMAGES), BF16),
            pltpu.VMEM((WIDE // LANES * REFS, LANES), F32),
        ]
        + [pltpu.VMEM((CELLS, LANES), F32)] * SUMS,
        compiler_params=pltpu.CompilerParams(vmem_limit_bytes=VMEM),
        name="bricks",
    )(cells, scale, *stats, expo, images, weights)


def brick_share(keep, send):
    voxels = keep.shape[1]
    x = keep + moved(send, ("core",), lambda c: (c + 1,))
    x = x.reshape(16, -1, voxels).astype(BF16)
    x = jnp.sum(lax.all_to_all(x, ("y", "xl", "xh"), 0, 0).astype(F32), axis=0)
    x = x.reshape(2, -1, voxels)
    x = x[0] + moved(x[1], ("z",), lambda z: (z ^ 4,))
    x = x.reshape(4, -1, voxels)
    return x[0] + sum([moved(x[k], ("z",), lambda z: (z ^ k,)) for k in (1, 2, 3)])


def body(images, img_scale, references, pattern, tile_owner, tile_brick, tile_block, weights):
    cut = 32
    at = {a: lax.axis_index(a) for a in AXES}
    owned = tile_owner.reshape(-1)
    codes = jnp.concatenate([owned, (tile_brick * 8 + tile_block).reshape(-1)])
    parts = gathered_references(references, codes, cut)

    code = parts[0][:, :, cut].astype(I32)
    code = code[..., : owned.size] * 128 + code[..., owned.size :]
    code = code.swapaxes(0, 1).reshape(REFS, -1).T.reshape(-1)
    block, row = code % 8, code // 8 % 4
    core, xh = code // 32 % 2, code // 64 % 2
    z, xl, y = code // 128 % 8, code // 1024 % 2, code // 2048
    away = ((jnp.bitwise_xor(core, at["core"]) * 4 + y) * 2 + xl) * 2 + xh
    away = away * 8 + jnp.bitwise_xor(z, at["z"])
    cells = block * (CELLS // 8) + away * 4 + row

    me = jnp.stack([at["y"], at["xl"]]).astype(I32)
    expo, stats = scores_of(me, images, img_scale[:, None], pattern, parts, cut)
    others = [
        moved(stats, ORI, lambda h, c: (h + dh, c + dc)) for dh, dc in ((0, 1), (1, 0), (1, 1))
    ]
    scale = img_scale.reshape(8, LANES)
    keep, send, evidence = bricks_of(cells, scale, (stats, *others), expo, images, weights)
    return brick_share(keep, send), evidence.reshape(-1)


def solution(mesh):
    cut_mesh = Mesh(mesh.devices.reshape(*AXES.values()), tuple(AXES))
    placed = (
        P(IMG, None),
        P(IMG),
        P(ORI, IMG),
        P(IMG, ORI),
        P(ORI, IMG, None),
        P(ORI, IMG),
        P(ORI, IMG),
        P(),
    )
    return jax.shard_map(
        body,
        mesh=cut_mesh,
        in_specs=placed,
        out_specs=(P(IMG + ORI, None), P(IMG)),
        check_vma=False,
    )
```

```python
import functools
import math

import jax
import jax.numpy as jnp
from jax import lax
from jax.experimental import pallas as pl
from jax.experimental.pallas import tpu as pltpu
from jax.sharding import Mesh
from jax.sharding import PartitionSpec as P

BF16, F32, I32 = jnp.bfloat16, jnp.float32, jnp.int32
AXES = {"y": 4, "xl": 2, "z": 8, "xh": 2, "core": 2}
IMG, ORI = ("y", "xl", "z"), ("xh", "core")
REFS, VALUES, IMAGES = 512, 4096, 1024
GROUP = REFS // 2
SHARE = 64
CELLS = 8192
LANES = 128
VMEM = 58 * 2**20


def moved(x, axes, target):
    sizes = [AXES[a] for a in axes]
    pairs = []
    for i in range(math.prod(sizes)):
        at, k = [], i
        for n in reversed(sizes):
            at.insert(0, k % n)
            k //= n
        to = 0
        for n, c in zip(sizes, target(*at)):
            to = to * n + c % n
        pairs.append((i, to))
    return lax.ppermute(x, axes, pairs)


def spread(x, axes):
    n = math.prod(AXES[a] for a in axes)
    return lax.all_to_all(jnp.broadcast_to(x[None], (n, *x.shape)), axes, 0, 0)


def gathered_references(references, codes):
    share = references.T
    near = spread(share[:, :GROUP], ("y", "xl"))
    first = lax.all_gather(near, "z", axis=0)
    more = jnp.pad(codes.astype(BF16).reshape(2, GROUP), ((0, 6), (0, 0)))
    own = spread(jnp.concatenate([share[:, GROUP:], more]), ("z",))
    codes = spread(own[:, SHARE : SHARE + 2].reshape(8, -1), ("y", "xl"))
    own = own[:, :SHARE]
    other = moved(own, ("xl",), lambda xl: (xl + 1,))
    near = [own] + [moved(own, ("y",), lambda y: (y + d,)) for d in (1, 2, 3)]
    far = [other] + [moved(other, ("y",), lambda y: (y + d,)) for d in (1, 3)]
    far.insert(2, moved(near[2], ("xl",), lambda xl: (xl + 1,)))
    return [first], near + far, codes.astype(I32)


def eye():
    return lax.broadcasted_iota(I32, (LANES, LANES), 0) == lax.broadcasted_iota(
        I32, (LANES, LANES), 1
    )


def scores_kernel(group, me, images, scale, pattern, before, *rest):
    *parts, expo, stats, refs, sems = rest
    step = pl.program_id(0)
    rows = images.shape[0]

    @pl.when(step == 0)
    def _():
        if len(parts) == 1:
            copies = [(parts[0].at[z], refs.at[:, z]) for z in range(8)]
        else:
            copies = []
            for i, part in enumerate(parts):
                y, xl = (me[0] + 4 - i % 4) % 4, (me[1] + i // 4) % 2
                copies.append((part, refs.at[y * 2 + xl]))
        copies = [pltpu.make_async_copy(a, b, sems.at[i]) for i, (a, b) in enumerate(copies)]
        for c in copies:
            c.start()
        if group:
            stats[0 : 16 * group, :] = before[0 : 16 * group, :]
        for c in copies:
            c.wait()

    total = jnp.dot(
        images[...], refs[...].reshape(VALUES, GROUP), preferred_element_type=F32
    )
    scores = total * scale[...] * (1.0 / math.sqrt(VALUES))
    active = pattern[:, group : group + 1] > 0
    masked = jnp.where(active, scores, -1e30)
    peak = jnp.max(masked, axis=1, keepdims=True)
    value = jnp.where(active, jnp.exp(masked - peak), 0.0)
    mass = jnp.sum(value, axis=1, keepdims=True)
    expo[...] = value.T
    for j in range(rows // LANES):
        part = slice(j * LANES, (j + 1) * LANES)
        at = step * (rows // LANES) + j
        for k, column in enumerate((peak, mass)):
            stats[pl.ds(16 * group + k * 8 + at, 1), :] = jnp.sum(
                jnp.where(eye(), column[part], 0.0), axis=0, keepdims=True
            )


def scores_of(group, me, images, scale, pattern, before, parts, rows=256):
    return pl.pallas_call(
        functools.partial(scores_kernel, group),
        grid=(IMAGES // rows,),
        in_specs=[
            pl.BlockSpec(memory_space=pltpu.SMEM),
            pl.BlockSpec((rows, VALUES), lambda i: (i, 0)),
            pl.BlockSpec((rows, 1), lambda i: (i, 0)),
            pl.BlockSpec((rows, 2), lambda i: (i, 0)),
            pl.BlockSpec((16, LANES), lambda i: (0, 0)),
        ]
        + [pl.BlockSpec(memory_space=pl.ANY)] * len(parts),
        out_specs=[
            pl.BlockSpec((GROUP, rows), lambda i: (0, i)),
            pl.BlockSpec((16 * group + 16, LANES), lambda i: (0, 0)),
        ],
        out_shape=[
            jax.ShapeDtypeStruct((GROUP, IMAGES), F32),
            jax.ShapeDtypeStruct((16 * group + 16, LANES), F32),
        ],
        scratch_shapes=[
            pltpu.VMEM((8, 8, SHARE, GROUP), BF16),
            pltpu.SemaphoreType.DMA((8,)),
        ],
        compiler_params=pltpu.CompilerParams(vmem_limit_bytes=VMEM),
        cost_estimate=pl.CostEstimate(
            flops=2 * IMAGES * VALUES * GROUP,
            bytes_accessed=2 * IMAGES * VALUES + 2 * VALUES * GROUP + 4 * IMAGES * GROUP,
            transcendentals=IMAGES * GROUP,
        ),
        name=f"scores{group}",
    )(me, images, scale, pattern, before, *parts)


UNROLL = 64
SUMS = 8
WIDE = 1024


def bricks_kernel(
    cells, scale, s0, s1, s2, s3, expo0, expo1, images, weights,
    keep, send, evidence, scaled, tiles, *sums,
):
    step = pl.program_id(0)

    @pl.when(step == 0)
    def _():
        pairs = [
            (s[16 * g : 16 * g + 8, :], s[16 * g + 8 : 16 * g + 16, :])
            for s in (s0, s1, s2, s3)
            for g in range(2)
        ]
        peak = functools.reduce(jnp.maximum, [p for p, _ in pairs])
        mass = sum(m * jnp.exp(p - peak) for p, m in pairs)
        evidence[...] = peak + jnp.log(mass)
        factors = [jnp.exp(pairs[g][0] - peak) / mass * scale[...] for g in range(2)]
        for j in range(IMAGES // LANES):
            part = slice(j * LANES, (j + 1) * LANES)
            for g, (expo, factor) in enumerate(zip((expo0, expo1), factors)):
                scaled[g * GROUP : (g + 1) * GROUP, part] = (
                    expo[:, part] * factor[j : j + 1, :]
                ).astype(BF16)

        def clear(i, _):
            for c in sums:
                c[pl.ds(i * 256, 256), :] = jnp.zeros((256, LANES), F32)
            return 0

        lax.fori_loop(0, CELLS // 256, clear, 0)

    for n in range(0, WIDE, 256):
        block = jnp.dot(scaled[...], images[:, n : n + 256], preferred_element_type=F32)
        for k in range(2):
            at = (n // LANES + k) * REFS
            tiles[at : at + REFS, :] = block[:, k * LANES : (k + 1) * LANES]

    count = tiles.shape[0]

    def add(i, _):
        for u in range(UNROLL):
            row = i * UNROLL + u
            cell = pl.ds(cells[row], 1)
            c = sums[u % SUMS]
            c[cell, :] = c[cell, :] + tiles[pl.ds(row, 1), :]
        return 0

    lax.fori_loop(0, count // UNROLL, add, 0)

    @pl.when(step == pl.num_programs(0) - 1)
    def _():
        for r in range(0, 1024, 256):
            total = jnp.zeros((256, weights.shape[2]), F32)
            for p in range(8):
                part = pl.ds(p * 1024 + r, 256)
                cell = functools.reduce(jnp.add, [c[part, :] for c in sums])
                high = cell.astype(BF16)
                low = (cell - high.astype(F32)).astype(BF16)
                w = weights[p]
                total += jnp.dot(
                    jnp.concatenate([high, low], axis=1),
                    jnp.concatenate([w, w], axis=0),
                    preferred_element_type=F32,
                )
            if r < 512:
                keep[r : r + 256, :] = total
            else:
                send[r - 512 : r - 256, :] = total


def bricks_of(cells, scale, stats, expos, images, weights):
    positions, width, voxels = weights.shape
    half = pl.BlockSpec((512, voxels), lambda i: (0, 0))
    return pl.pallas_call(
        bricks_kernel,
        grid=(VALUES // WIDE,),
        in_specs=[
            pl.BlockSpec(
                (WIDE // LANES * REFS,), lambda i: (i,), memory_space=pltpu.SMEM
            ),
            pl.BlockSpec((8, LANES), lambda i: (0, 0)),
            *[pl.BlockSpec((32, LANES), lambda i: (0, 0))] * 4,
            *[pl.BlockSpec((GROUP, IMAGES), lambda i: (0, 0))] * 2,
            pl.BlockSpec((IMAGES, WIDE), lambda i: (0, i)),
            pl.BlockSpec((positions, width, voxels), lambda i: (0, 0, 0)),
        ],
        out_specs=[half, half, pl.BlockSpec((8, LANES), lambda i: (0, 0))],
        out_shape=[
            jax.ShapeDtypeStruct((512, voxels), F32),
            jax.ShapeDtypeStruct((512, voxels), F32),
            jax.ShapeDtypeStruct((8, LANES), F32),
        ],
        scratch_shapes=[
            pltpu.VMEM((REFS, IMAGES), BF16),
            pltpu.VMEM((WIDE // LANES * REFS, LANES), F32),
        ]
        + [pltpu.VMEM((CELLS, LANES), F32)] * SUMS,
        compiler_params=pltpu.CompilerParams(vmem_limit_bytes=VMEM),
        name="bricks",
    )(cells, scale, *stats, *expos, images, weights)


def brick_share(keep, send):
    voxels = keep.shape[1]
    x = keep + moved(send, ("core",), lambda c: (c + 1,))
    x = x.reshape(16, -1, voxels).astype(BF16)
    x = jnp.sum(lax.all_to_all(x, ("y", "xl", "xh"), 0, 0).astype(F32), axis=0)
    x = x.reshape(2, -1, voxels)
    x = x[0] + moved(x[1], ("z",), lambda z: (z ^ 4,))
    x = x.reshape(4, -1, voxels)
    return x[0] + sum([moved(x[k], ("z",), lambda z: (z ^ k,)) for k in (1, 2, 3)])


def body(images, img_scale, references, pattern, tile_owner, tile_brick, tile_block, weights):
    at = {a: lax.axis_index(a) for a in AXES}
    owned = tile_owner.reshape(-1)
    codes = jnp.concatenate([owned, (tile_brick * 8 + tile_block).reshape(-1)])
    first, second, code = gathered_references(references, codes)

    code = code[..., : owned.size] * 128 + code[..., owned.size :]
    code = code.reshape(REFS, -1).T.reshape(-1)
    block, row = code % 8, code // 8 % 4
    core, xh = code // 32 % 2, code // 64 % 2
    z, xl, y = code // 128 % 8, code // 1024 % 2, code // 2048
    away = ((jnp.bitwise_xor(core, at["core"]) * 4 + y) * 2 + xl) * 2 + xh
    away = away * 8 + jnp.bitwise_xor(z, at["z"])
    cells = block * (CELLS // 8) + away * 4 + row

    me = jnp.stack([at["y"], at["xl"]]).astype(I32)
    column = img_scale[:, None]
    none = jnp.zeros((16, LANES), F32)
    expo0, stats = scores_of(0, me, images, column, pattern, none, first)
    expo1, stats = scores_of(1, me, images, column, pattern, stats, second)
    others = [
        moved(stats, ORI, lambda h, c: (h + dh, c + dc)) for dh, dc in ((0, 1), (1, 0), (1, 1))
    ]
    scale = img_scale.reshape(8, LANES)
    keep, send, evidence = bricks_of(cells, scale, (stats, *others), (expo0, expo1), images, weights)
    return brick_share(keep, send), evidence.reshape(-1)


def solution(mesh):
    cut_mesh = Mesh(mesh.devices.reshape(*AXES.values()), tuple(AXES))
    placed = (
        P(IMG, None),
        P(IMG),
        P(ORI, IMG),
        P(IMG, ORI),
        P(ORI, IMG, None),
        P(ORI, IMG),
        P(ORI, IMG),
        P(),
    )
    return jax.shard_map(
        body,
        mesh=cut_mesh,
        in_specs=placed,
        out_specs=(P(IMG + ORI, None), P(IMG)),
        check_vma=False,
    )
```

```python
import functools
import math

import jax
import jax.numpy as jnp
from jax import lax
from jax.experimental import pallas as pl
from jax.experimental.pallas import tpu as pltpu
from jax.sharding import Mesh
from jax.sharding import PartitionSpec as P

BF16, F32, I32 = jnp.bfloat16, jnp.float32, jnp.int32
AXES = {"y": 4, "xl": 2, "z": 8, "xh": 2, "core": 2}
IMG, ORI = ("y", "xl", "z"), ("xh", "core")
REFS, VALUES, IMAGES = 512, 4096, 1024
SHARE = 64
CELLS = 8192
LANES = 128
VMEM = 58 * 2**20


def moved(x, axes, target):
    sizes = [AXES[a] for a in axes]
    pairs = []
    for i in range(math.prod(sizes)):
        at, k = [], i
        for n in reversed(sizes):
            at.insert(0, k % n)
            k //= n
        to = 0
        for n, c in zip(sizes, target(*at)):
            to = to * n + c % n
        pairs.append((i, to))
    return lax.ppermute(x, axes, pairs)


def spread(x, axes):
    n = math.prod(AXES[a] for a in axes)
    return lax.all_to_all(jnp.broadcast_to(x[None], (n, *x.shape)), axes, 0, 0)


def gathered_references(references, codes, cut):
    share = references.T
    more = jnp.pad(codes.astype(BF16)[None], ((0, 7), (0, 0)))
    near = spread(jnp.concatenate([share[:cut], more]), ("y", "xl"))
    ended_z = lax.all_gather(near, "z", axis=0)
    own = spread(share[cut:], ("z",))
    other = moved(own, ("xl",), lambda xl: (xl + 1,))
    near = [own] + [moved(own, ("y",), lambda y: (y + d,)) for d in (1, 2, 3)]
    far = [other] + [moved(other, ("y",), lambda y: (y + d,)) for d in (1, 3)]
    far.insert(2, moved(near[2], ("xl",), lambda xl: (xl + 1,)))
    return [ended_z, *near, *far]


def eye():
    return lax.broadcasted_iota(I32, (LANES, LANES), 0) == lax.broadcasted_iota(
        I32, (LANES, LANES), 1
    )


def scores_kernel(
    cut, me, images, scale, pattern, by_z, a0, a1, a2, a3, b0, b1, b2, b3, expo, stats, refs, sems
):
    step = pl.program_id(0)
    rows = images.shape[0]

    @pl.when(step == 0)
    def _():
        copies = [(by_z.at[z, :, pl.ds(0, cut)], refs.at[:, z, pl.ds(0, cut)]) for z in range(8)]
        for i, part in enumerate((a0, a1, a2, a3, b0, b1, b2, b3)):
            y, xl = (me[0] + 4 - i % 4) % 4, (me[1] + i // 4) % 2
            copies.append((part, refs.at[y * 2 + xl, :, pl.ds(cut, SHARE - cut)]))
        for i, (a, b) in enumerate(copies):
            pltpu.make_async_copy(a, b, sems.at[i]).start()
        for i, (a, b) in enumerate(copies):
            pltpu.make_async_copy(a, b, sems.at[i]).wait()

    total = jnp.dot(
        images[...], refs[...].reshape(VALUES, REFS), preferred_element_type=F32
    )
    scores = total * scale[...] * (1.0 / math.sqrt(VALUES))
    group = lax.broadcasted_iota(I32, (rows, REFS), 1) // (REFS // 2)
    flags = pattern[...]
    active = jnp.where(group == 0, flags[:, 0:1], flags[:, 1:2]) > 0
    masked = jnp.where(active, scores, -1e30)
    peak = jnp.max(masked, axis=1, keepdims=True)
    value = jnp.where(active, jnp.exp(masked - peak), 0.0)
    mass = jnp.sum(value, axis=1, keepdims=True)
    expo[...] = value.T
    for j in range(rows // LANES):
        part = slice(j * LANES, (j + 1) * LANES)
        at = step * (rows // LANES) + j
        for k, column in enumerate((peak, mass)):
            stats[pl.ds(k * 8 + at, 1), :] = jnp.sum(
                jnp.where(eye(), column[part], 0.0), axis=0, keepdims=True
            )


def scores_of(me, images, scale, pattern, parts, cut, rows=256):
    return pl.pallas_call(
        functools.partial(scores_kernel, cut),
        grid=(IMAGES // rows,),
        in_specs=[
            pl.BlockSpec(memory_space=pltpu.SMEM),
            pl.BlockSpec((rows, VALUES), lambda i: (i, 0)),
            pl.BlockSpec((rows, 1), lambda i: (i, 0)),
            pl.BlockSpec((rows, 2), lambda i: (i, 0)),
        ]
        + [pl.BlockSpec(memory_space=pl.ANY)] * len(parts),
        out_specs=[
            pl.BlockSpec((REFS, rows), lambda i: (0, i)),
            pl.BlockSpec((16, LANES), lambda i: (0, 0)),
        ],
        out_shape=[
            jax.ShapeDtypeStruct((REFS, IMAGES), F32),
            jax.ShapeDtypeStruct((16, LANES), F32),
        ],
        scratch_shapes=[
            pltpu.VMEM((8, 8, SHARE, REFS), BF16),
            pltpu.SemaphoreType.DMA((16,)),
        ],
        compiler_params=pltpu.CompilerParams(vmem_limit_bytes=VMEM),
        name="scores",
    )(me, images, scale, pattern, *parts)


UNROLL = 64
SUMS = 8
WIDE = 1024


def bricks_kernel(
    cells, scale, s0, s1, s2, s3, expo, images, weights,
    keep, send, evidence, scaled, tiles, *sums,
):
    step = pl.program_id(0)

    @pl.when(step == 0)
    def _():
        pairs = [(s[0:8, :], s[8:16, :]) for s in (s0, s1, s2, s3)]
        peak = functools.reduce(jnp.maximum, [p for p, _ in pairs])
        mass = sum(m * jnp.exp(p - peak) for p, m in pairs)
        evidence[...] = peak + jnp.log(mass)
        factor = jnp.exp(pairs[0][0] - peak) / mass * scale[...]
        for j in range(IMAGES // LANES):
            part = slice(j * LANES, (j + 1) * LANES)
            scaled[:, part] = (expo[:, part] * factor[j : j + 1, :]).astype(BF16)

        def clear(i, _):
            for c in sums:
                c[pl.ds(i * 256, 256), :] = jnp.zeros((256, LANES), F32)
            return 0

        lax.fori_loop(0, CELLS // 256, clear, 0)

    for n in range(0, WIDE, 256):
        block = jnp.dot(scaled[...], images[:, n : n + 256], preferred_element_type=F32)
        for k in range(2):
            at = (n // LANES + k) * REFS
            tiles[at : at + REFS, :] = block[:, k * LANES : (k + 1) * LANES]

    count = tiles.shape[0]

    def add(i, _):
        for u in range(UNROLL):
            row = i * UNROLL + u
            cell = pl.ds(cells[row], 1)
            c = sums[u % SUMS]
            c[cell, :] = c[cell, :] + tiles[pl.ds(row, 1), :]
        return 0

    lax.fori_loop(0, count // UNROLL, add, 0)

    @pl.when(step == pl.num_programs(0) - 1)
    def _():
        for r in range(0, 1024, 256):
            total = jnp.zeros((256, weights.shape[2]), F32)
            for p in range(8):
                part = pl.ds(p * 1024 + r, 256)
                cell = functools.reduce(jnp.add, [c[part, :] for c in sums])
                high = cell.astype(BF16)
                low = (cell - high.astype(F32)).astype(BF16)
                w = weights[p]
                total += jnp.dot(
                    jnp.concatenate([high, low], axis=1),
                    jnp.concatenate([w, w], axis=0),
                    preferred_element_type=F32,
                )
            if r < 512:
                keep[r : r + 256, :] = total
            else:
                send[r - 512 : r - 256, :] = total


def bricks_of(cells, scale, stats, expo, images, weights):
    positions, width, voxels = weights.shape
    half = pl.BlockSpec((512, voxels), lambda i: (0, 0))
    return pl.pallas_call(
        bricks_kernel,
        grid=(VALUES // WIDE,),
        in_specs=[
            pl.BlockSpec(
                (WIDE // LANES * REFS,), lambda i: (i,), memory_space=pltpu.SMEM
            ),
            pl.BlockSpec((8, LANES), lambda i: (0, 0)),
            *[pl.BlockSpec((16, LANES), lambda i: (0, 0))] * 4,
            pl.BlockSpec((REFS, IMAGES), lambda i: (0, 0)),
            pl.BlockSpec((IMAGES, WIDE), lambda i: (0, i)),
            pl.BlockSpec((positions, width, voxels), lambda i: (0, 0, 0)),
        ],
        out_specs=[half, half, pl.BlockSpec((8, LANES), lambda i: (0, 0))],
        out_shape=[
            jax.ShapeDtypeStruct((512, voxels), F32),
            jax.ShapeDtypeStruct((512, voxels), F32),
            jax.ShapeDtypeStruct((8, LANES), F32),
        ],
        scratch_shapes=[
            pltpu.VMEM((REFS, IMAGES), BF16),
            pltpu.VMEM((WIDE // LANES * REFS, LANES), F32),
        ]
        + [pltpu.VMEM((CELLS, LANES), F32)] * SUMS,
        compiler_params=pltpu.CompilerParams(vmem_limit_bytes=VMEM),
        name="bricks",
    )(cells, scale, *stats, expo, images, weights)


def brick_share(keep, send):
    voxels = keep.shape[1]
    x = keep + moved(send, ("core",), lambda c: (c + 1,))
    x = x.reshape(16, -1, voxels).astype(BF16)
    x = jnp.sum(lax.all_to_all(x, ("y", "xl", "xh"), 0, 0).astype(F32), axis=0)
    x = x.reshape(2, -1, voxels)
    x = x[0] + moved(x[1], ("z",), lambda z: (z ^ 4,))
    x = x.reshape(4, -1, voxels)
    return x[0] + sum([moved(x[k], ("z",), lambda z: (z ^ k,)) for k in (1, 2, 3)])


def body(images, img_scale, references, pattern, tile_owner, tile_brick, tile_block, weights):
    cut = 32
    at = {a: lax.axis_index(a) for a in AXES}
    owned = tile_owner.reshape(-1)
    codes = jnp.concatenate([owned, (tile_brick * 8 + tile_block).reshape(-1)])
    parts = gathered_references(references, codes, cut)

    code = parts[0][:, :, cut].astype(I32)
    code = code[..., : owned.size] * 128 + code[..., owned.size :]
    code = code.swapaxes(0, 1).reshape(REFS, -1).T.reshape(-1)
    block, row = code % 8, code // 8 % 4
    core, xh = code // 32 % 2, code // 64 % 2
    z, xl, y = code // 128 % 8, code // 1024 % 2, code // 2048
    away = ((jnp.bitwise_xor(core, at["core"]) * 4 + y) * 2 + xl) * 2 + xh
    away = away * 8 + jnp.bitwise_xor(z, at["z"])
    cells = block * (CELLS // 8) + away * 4 + row

    me = jnp.stack([at["y"], at["xl"]]).astype(I32)
    expo, stats = scores_of(me, images, img_scale[:, None], pattern, parts, cut)
    others = [
        moved(stats, ORI, lambda h, c: (h + dh, c + dc)) for dh, dc in ((0, 1), (1, 0), (1, 1))
    ]
    scale = img_scale.reshape(8, LANES)
    keep, send, evidence = bricks_of(cells, scale, (stats, *others), expo, images, weights)
    return brick_share(keep, send), evidence.reshape(-1)


def solution(mesh):
    cut_mesh = Mesh(mesh.devices.reshape(*AXES.values()), tuple(AXES))
    placed = (
        P(IMG, None),
        P(IMG),
        P(ORI, IMG),
        P(IMG, ORI),
        P(ORI, IMG, None),
        P(ORI, IMG),
        P(ORI, IMG),
        P(),
    )
    return jax.shard_map(
        body,
        mesh=cut_mesh,
        in_specs=placed,
        out_specs=(P(IMG + ORI, None), P(IMG)),
        check_vma=False,
    )
```

```python
import functools
import math

import jax
import jax.numpy as jnp
from jax import lax
from jax.experimental import pallas as pl
from jax.experimental.pallas import tpu as pltpu
from jax.sharding import Mesh
from jax.sharding import PartitionSpec as P

BF16, F32, I32 = jnp.bfloat16, jnp.float32, jnp.int32
AXES = {"y": 4, "xl": 2, "z": 8, "xh": 2, "core": 2}
IMG, ORI = ("y", "xl", "z"), ("xh", "core")
REFS, VALUES, IMAGES = 512, 4096, 1024
SHARE = 64
CELLS = 8192
LANES = 128
VMEM = 58 * 2**20


def moved(x, axes, target):
    sizes = [AXES[a] for a in axes]
    pairs = []
    for i in range(math.prod(sizes)):
        at, k = [], i
        for n in reversed(sizes):
            at.insert(0, k % n)
            k //= n
        to = 0
        for n, c in zip(sizes, target(*at)):
            to = to * n + c % n
        pairs.append((i, to))
    return lax.ppermute(x, axes, pairs)


def spread(x, axes):
    n = math.prod(AXES[a] for a in axes)
    return lax.all_to_all(jnp.broadcast_to(x[None], (n, *x.shape)), axes, 0, 0)


def gathered_references(references, codes, cut):
    share = references.T
    near = spread(share[:cut], ("y", "xl"))
    ended_z = lax.all_gather(near, "z", axis=0)
    more = jnp.pad(codes.astype(BF16)[None], ((0, 7), (0, 0)))
    own = spread(jnp.concatenate([share[cut:], more]), ("z",))
    codes, own = own[:, SHARE - cut], own[:, : SHARE - cut]
    other = moved(own, ("xl",), lambda xl: (xl + 1,))
    near = [own] + [moved(own, ("y",), lambda y: (y + d,)) for d in (1, 2, 3)]
    far = [other] + [moved(other, ("y",), lambda y: (y + d,)) for d in (1, 3)]
    far.insert(2, moved(near[2], ("xl",), lambda xl: (xl + 1,)))
    codes, _ = lax.optimization_barrier((codes, other))
    codes = spread(codes, ("y", "xl")).astype(I32)
    return [ended_z, *near, *far], codes


def eye():
    return lax.broadcasted_iota(I32, (LANES, LANES), 0) == lax.broadcasted_iota(
        I32, (LANES, LANES), 1
    )


def scores_kernel(
    cut, me, images, scale, pattern, by_z, a0, a1, a2, a3, b0, b1, b2, b3, expo, stats, refs, sems
):
    step = pl.program_id(0)
    rows = images.shape[0]

    @pl.when(step == 0)
    def _():
        copies = [(by_z.at[z], refs.at[:, z, pl.ds(0, cut)]) for z in range(8)]
        for i, part in enumerate((a0, a1, a2, a3, b0, b1, b2, b3)):
            y, xl = (me[0] + 4 - i % 4) % 4, (me[1] + i // 4) % 2
            copies.append((part, refs.at[y * 2 + xl, :, pl.ds(cut, SHARE - cut)]))
        for i, (a, b) in enumerate(copies):
            pltpu.make_async_copy(a, b, sems.at[i]).start()
        for i, (a, b) in enumerate(copies):
            pltpu.make_async_copy(a, b, sems.at[i]).wait()

    total = jnp.dot(
        images[...], refs[...].reshape(VALUES, REFS), preferred_element_type=F32
    )
    scores = total * scale[...] * (1.0 / math.sqrt(VALUES))
    group = lax.broadcasted_iota(I32, (rows, REFS), 1) // (REFS // 2)
    flags = pattern[...]
    active = jnp.where(group == 0, flags[:, 0:1], flags[:, 1:2]) > 0
    masked = jnp.where(active, scores, -1e30)
    peak = jnp.max(masked, axis=1, keepdims=True)
    value = jnp.where(active, jnp.exp(masked - peak), 0.0)
    mass = jnp.sum(value, axis=1, keepdims=True)
    expo[...] = value.T
    for j in range(rows // LANES):
        part = slice(j * LANES, (j + 1) * LANES)
        at = step * (rows // LANES) + j
        for k, column in enumerate((peak, mass)):
            stats[pl.ds(k * 8 + at, 1), :] = jnp.sum(
                jnp.where(eye(), column[part], 0.0), axis=0, keepdims=True
            )


def scores_of(me, images, scale, pattern, parts, cut, rows=256):
    return pl.pallas_call(
        functools.partial(scores_kernel, cut),
        grid=(IMAGES // rows,),
        in_specs=[
            pl.BlockSpec(memory_space=pltpu.SMEM),
            pl.BlockSpec((rows, VALUES), lambda i: (i, 0)),
            pl.BlockSpec((rows, 1), lambda i: (i, 0)),
            pl.BlockSpec((rows, 2), lambda i: (i, 0)),
        ]
        + [pl.BlockSpec(memory_space=pl.ANY)] * len(parts),
        out_specs=[
            pl.BlockSpec((REFS, rows), lambda i: (0, i)),
            pl.BlockSpec((16, LANES), lambda i: (0, 0)),
        ],
        out_shape=[
            jax.ShapeDtypeStruct((REFS, IMAGES), F32),
            jax.ShapeDtypeStruct((16, LANES), F32),
        ],
        scratch_shapes=[
            pltpu.VMEM((8, 8, SHARE, REFS), BF16),
            pltpu.SemaphoreType.DMA((16,)),
        ],
        compiler_params=pltpu.CompilerParams(vmem_limit_bytes=VMEM),
        name="scores",
    )(me, images, scale, pattern, *parts)


UNROLL = 64
SUMS = 8
WIDE = 1024


def bricks_kernel(
    cells, scale, s0, s1, s2, s3, expo, images, weights,
    keep, send, evidence, scaled, tiles, *sums,
):
    step = pl.program_id(0)

    @pl.when(step == 0)
    def _():
        pairs = [(s[0:8, :], s[8:16, :]) for s in (s0, s1, s2, s3)]
        peak = functools.reduce(jnp.maximum, [p for p, _ in pairs])
        mass = sum(m * jnp.exp(p - peak) for p, m in pairs)
        evidence[...] = peak + jnp.log(mass)
        factor = jnp.exp(pairs[0][0] - peak) / mass * scale[...]
        for j in range(IMAGES // LANES):
            part = slice(j * LANES, (j + 1) * LANES)
            scaled[:, part] = (expo[:, part] * factor[j : j + 1, :]).astype(BF16)

        def clear(i, _):
            for c in sums:
                c[pl.ds(i * 256, 256), :] = jnp.zeros((256, LANES), F32)
            return 0

        lax.fori_loop(0, CELLS // 256, clear, 0)

    for n in range(0, WIDE, 256):
        block = jnp.dot(scaled[...], images[:, n : n + 256], preferred_element_type=F32)
        for k in range(2):
            at = (n // LANES + k) * REFS
            tiles[at : at + REFS, :] = block[:, k * LANES : (k + 1) * LANES]

    count = tiles.shape[0]

    def add(i, _):
        for u in range(UNROLL):
            row = i * UNROLL + u
            cell = pl.ds(cells[row], 1)
            c = sums[u % SUMS]
            c[cell, :] = c[cell, :] + tiles[pl.ds(row, 1), :]
        return 0

    lax.fori_loop(0, count // UNROLL, add, 0)

    @pl.when(step == pl.num_programs(0) - 1)
    def _():
        for r in range(0, 1024, 256):
            total = jnp.zeros((256, weights.shape[2]), F32)
            for p in range(8):
                part = pl.ds(p * 1024 + r, 256)
                cell = functools.reduce(jnp.add, [c[part, :] for c in sums])
                high = cell.astype(BF16)
                low = (cell - high.astype(F32)).astype(BF16)
                w = weights[p]
                total += jnp.dot(
                    jnp.concatenate([high, low], axis=1),
                    jnp.concatenate([w, w], axis=0),
                    preferred_element_type=F32,
                )
            if r < 512:
                keep[r : r + 256, :] = total
            else:
                send[r - 512 : r - 256, :] = total


def bricks_of(cells, scale, stats, expo, images, weights):
    positions, width, voxels = weights.shape
    half = pl.BlockSpec((512, voxels), lambda i: (0, 0))
    return pl.pallas_call(
        bricks_kernel,
        grid=(VALUES // WIDE,),
        in_specs=[
            pl.BlockSpec(
                (WIDE // LANES * REFS,), lambda i: (i,), memory_space=pltpu.SMEM
            ),
            pl.BlockSpec((8, LANES), lambda i: (0, 0)),
            *[pl.BlockSpec((16, LANES), lambda i: (0, 0))] * 4,
            pl.BlockSpec((REFS, IMAGES), lambda i: (0, 0)),
            pl.BlockSpec((IMAGES, WIDE), lambda i: (0, i)),
            pl.BlockSpec((positions, width, voxels), lambda i: (0, 0, 0)),
        ],
        out_specs=[half, half, pl.BlockSpec((8, LANES), lambda i: (0, 0))],
        out_shape=[
            jax.ShapeDtypeStruct((512, voxels), F32),
            jax.ShapeDtypeStruct((512, voxels), F32),
            jax.ShapeDtypeStruct((8, LANES), F32),
        ],
        scratch_shapes=[
            pltpu.VMEM((REFS, IMAGES), BF16),
            pltpu.VMEM((WIDE // LANES * REFS, LANES), F32),
        ]
        + [pltpu.VMEM((CELLS, LANES), F32)] * SUMS,
        compiler_params=pltpu.CompilerParams(vmem_limit_bytes=VMEM),
        name="bricks",
    )(cells, scale, *stats, expo, images, weights)


def brick_share(keep, send):
    voxels = keep.shape[1]
    x = keep + moved(send, ("core",), lambda c: (c + 1,))
    x = x.reshape(16, -1, voxels).astype(BF16)
    x = jnp.sum(lax.all_to_all(x, ("y", "xl", "xh"), 0, 0).astype(F32), axis=0)
    x = x.reshape(2, -1, voxels)
    x = x[0] + moved(x[1], ("z",), lambda z: (z ^ 4,))
    x = x.reshape(4, -1, voxels)
    return x[0] + sum([moved(x[k], ("z",), lambda z: (z ^ k,)) for k in (1, 2, 3)])


def body(images, img_scale, references, pattern, tile_owner, tile_brick, tile_block, weights):
    cut = 32
    at = {a: lax.axis_index(a) for a in AXES}
    owned = tile_owner.reshape(-1)
    codes = jnp.concatenate([owned, (tile_brick * 8 + tile_block).reshape(-1)])
    parts, code = gathered_references(references, codes, cut)

    code = code[..., : owned.size] * 128 + code[..., owned.size :]
    code = code.reshape(REFS, -1).T.reshape(-1)
    block, row = code % 8, code // 8 % 4
    core, xh = code // 32 % 2, code // 64 % 2
    z, xl, y = code // 128 % 8, code // 1024 % 2, code // 2048
    away = ((jnp.bitwise_xor(core, at["core"]) * 4 + y) * 2 + xl) * 2 + xh
    away = away * 8 + jnp.bitwise_xor(z, at["z"])
    cells = block * (CELLS // 8) + away * 4 + row

    me = jnp.stack([at["y"], at["xl"]]).astype(I32)
    expo, stats = scores_of(me, images, img_scale[:, None], pattern, parts, cut)
    others = [
        moved(stats, ORI, lambda h, c: (h + dh, c + dc)) for dh, dc in ((0, 1), (1, 0), (1, 1))
    ]
    scale = img_scale.reshape(8, LANES)
    keep, send, evidence = bricks_of(cells, scale, (stats, *others), expo, images, weights)
    return brick_share(keep, send), evidence.reshape(-1)


def solution(mesh):
    cut_mesh = Mesh(mesh.devices.reshape(*AXES.values()), tuple(AXES))
    placed = (
        P(IMG, None),
        P(IMG),
        P(ORI, IMG),
        P(IMG, ORI),
        P(ORI, IMG, None),
        P(ORI, IMG),
        P(ORI, IMG),
        P(),
    )
    return jax.shard_map(
        body,
        mesh=cut_mesh,
        in_specs=placed,
        out_specs=(P(IMG + ORI, None), P(IMG)),
        check_vma=False,
    )
```

```python
import functools
import math

import jax
import jax.numpy as jnp
from jax import lax
from jax.experimental import pallas as pl
from jax.experimental.pallas import tpu as pltpu
from jax.sharding import Mesh
from jax.sharding import PartitionSpec as P

BF16, F32, I32 = jnp.bfloat16, jnp.float32, jnp.int32
AXES = {"y": 4, "xl": 2, "z": 8, "xh": 2, "core": 2}
IMG, ORI = ("y", "xl", "z"), ("xh", "core")
REFS, VALUES, IMAGES = 512, 4096, 1024
SHARE = 64
CELLS = 8192
LANES = 128
VMEM = 58 * 2**20


def moved(x, axes, target):
    sizes = [AXES[a] for a in axes]
    pairs = []
    for i in range(math.prod(sizes)):
        at, k = [], i
        for n in reversed(sizes):
            at.insert(0, k % n)
            k //= n
        to = 0
        for n, c in zip(sizes, target(*at)):
            to = to * n + c % n
        pairs.append((i, to))
    return lax.ppermute(x, axes, pairs)


def spread(x, axes):
    n = math.prod(AXES[a] for a in axes)
    return lax.all_to_all(jnp.broadcast_to(x[None], (n, *x.shape)), axes, 0, 0)


def gathered_references(references, codes, cut):
    share = references.T
    near = spread(share[:cut], ("y", "xl"))
    ended_z = lax.all_gather(near, "z", axis=0)
    more = jnp.pad(codes.astype(BF16)[None], ((0, 7), (0, 0)))
    own = spread(jnp.concatenate([share[cut:], more]), ("z",))
    codes, own = own[:, SHARE - cut], own[:, : SHARE - cut]
    other = moved(own, ("xl",), lambda xl: (xl + 1,))
    near = [own] + [moved(own, ("y",), lambda y: (y + d,)) for d in (1, 2, 3)]
    far = [other] + [moved(other, ("y",), lambda y: (y + d,)) for d in (1, 3)]
    far.insert(2, moved(near[2], ("xl",), lambda xl: (xl + 1,)))
    codes, _ = lax.optimization_barrier((codes, other))
    codes = spread(codes, ("y", "xl")).astype(I32)
    return [ended_z, *near, *far], codes


def eye():
    return lax.broadcasted_iota(I32, (LANES, LANES), 0) == lax.broadcasted_iota(
        I32, (LANES, LANES), 1
    )


DEEP = 1024


def scores_kernel(
    cut, me, images, scale, pattern, by_z, a0, a1, a2, a3, b0, b1, b2, b3,
    expo, stats, refs, total, sems,
):
    step = pl.program_id(0)
    each = DEEP // (8 * SHARE)

    def by_y(i, part):
        y, xl = (me[0] + 4 - i % 4) % 4, (me[1] + i // 4) % 2
        there = refs.at[y * 2 + xl, :, pl.ds(cut, SHARE - cut)]
        return pltpu.make_async_copy(part, there, sems.at[8 + i])

    def of_z(q):
        return pltpu.make_async_copy(
            by_z.at[:, q], refs.at[q, :, pl.ds(0, cut)], sems.at[q]
        )

    @pl.when(step == 0)
    def _():
        copies = [by_y(i, p) for i, p in enumerate((a0, a1, a2, a3, b0, b1, b2, b3))]
        for c in copies:
            c.start()
        for q in range(8):
            of_z(q).start()
        for c in copies:
            c.wait()

    for k in range(each):
        of_z(step * each + k).wait()
    part = jnp.dot(
        images[...],
        refs[pl.ds(step * each, each)].reshape(DEEP, REFS),
        preferred_element_type=F32,
    )

    @pl.when(step == 0)
    def _():
        total[...] = part

    @pl.when(step > 0)
    def _():
        total[...] = total[...] + part

    @pl.when(step == pl.num_programs(0) - 1)
    def _():
        rows = 256
        group = lax.broadcasted_iota(I32, (rows, REFS), 1) // (REFS // 2)
        for r in range(0, IMAGES, rows):
            here = slice(r, r + rows)
            scores = total[here, :] * scale[here, :] * (1.0 / math.sqrt(VALUES))
            flags = pattern[here, :]
            active = jnp.where(group == 0, flags[:, 0:1], flags[:, 1:2]) > 0
            masked = jnp.where(active, scores, -1e30)
            peak = jnp.max(masked, axis=1, keepdims=True)
            value = jnp.where(active, jnp.exp(masked - peak), 0.0)
            mass = jnp.sum(value, axis=1, keepdims=True)
            expo[:, here] = value.T
            for j in range(rows // LANES):
                cut_rows = slice(j * LANES, (j + 1) * LANES)
                at = r // LANES + j
                for k, column in enumerate((peak, mass)):
                    stats[k * 8 + at : k * 8 + at + 1, :] = jnp.sum(
                        jnp.where(eye(), column[cut_rows], 0.0), axis=0, keepdims=True
                    )


def scores_of(me, images, scale, pattern, parts, cut):
    return pl.pallas_call(
        functools.partial(scores_kernel, cut),
        grid=(VALUES // DEEP,),
        in_specs=[
            pl.BlockSpec(memory_space=pltpu.SMEM),
            pl.BlockSpec((IMAGES, DEEP), lambda i: (0, i)),
            pl.BlockSpec((IMAGES, 1), lambda i: (0, 0)),
            pl.BlockSpec((IMAGES, 2), lambda i: (0, 0)),
        ]
        + [pl.BlockSpec(memory_space=pl.ANY)] * len(parts),
        out_specs=[
            pl.BlockSpec((REFS, IMAGES), lambda i: (0, 0)),
            pl.BlockSpec((16, LANES), lambda i: (0, 0)),
        ],
        out_shape=[
            jax.ShapeDtypeStruct((REFS, IMAGES), F32),
            jax.ShapeDtypeStruct((16, LANES), F32),
        ],
        scratch_shapes=[
            pltpu.VMEM((8, 8, SHARE, REFS), BF16),
            pltpu.VMEM((IMAGES, REFS), F32),
            pltpu.SemaphoreType.DMA((16,)),
        ],
        compiler_params=pltpu.CompilerParams(vmem_limit_bytes=VMEM),
        name="scores",
    )(me, images, scale, pattern, *parts)


UNROLL = 128
SUMS = 8
WIDE = 1024


def bricks_kernel(
    cells, scale, s0, s1, s2, s3, expo, images, weights,
    keep, send, evidence, scaled, tiles, *sums,
):
    step = pl.program_id(0)

    @pl.when(step == 0)
    def _():
        pairs = [(s[0:8, :], s[8:16, :]) for s in (s0, s1, s2, s3)]
        peak = functools.reduce(jnp.maximum, [p for p, _ in pairs])
        mass = sum(m * jnp.exp(p - peak) for p, m in pairs)
        evidence[...] = peak + jnp.log(mass)
        factor = jnp.exp(pairs[0][0] - peak) / mass * scale[...]
        for j in range(IMAGES // LANES):
            part = slice(j * LANES, (j + 1) * LANES)
            scaled[:, part] = (expo[:, part] * factor[j : j + 1, :]).astype(BF16)

        def clear(i, _):
            for c in sums:
                c[pl.ds(i * 256, 256), :] = jnp.zeros((256, LANES), F32)
            return 0

        lax.fori_loop(0, CELLS // 256, clear, 0)

    for n in range(0, WIDE, 256):
        block = jnp.dot(scaled[...], images[:, n : n + 256], preferred_element_type=F32)
        for k in range(2):
            at = (n // LANES + k) * REFS
            tiles[at : at + REFS, :] = block[:, k * LANES : (k + 1) * LANES]

    count = tiles.shape[0]

    def add(i, _):
        for u in range(UNROLL):
            row = i * UNROLL + u
            cell = pl.ds(cells[row], 1)
            c = sums[u % SUMS]
            c[cell, :] = c[cell, :] + tiles[pl.ds(row, 1), :]
        return 0

    lax.fori_loop(0, count // UNROLL, add, 0)

    @pl.when(step == pl.num_programs(0) - 1)
    def _():
        for r in range(0, 1024, 256):
            total = jnp.zeros((256, weights.shape[2]), F32)
            for p in range(8):
                part = pl.ds(p * 1024 + r, 256)
                cell = functools.reduce(jnp.add, [c[part, :] for c in sums])
                high = cell.astype(BF16)
                low = (cell - high.astype(F32)).astype(BF16)
                w = weights[p]
                total += jnp.dot(
                    jnp.concatenate([high, low], axis=1),
                    jnp.concatenate([w, w], axis=0),
                    preferred_element_type=F32,
                )
            if r < 512:
                keep[r : r + 256, :] = total
            else:
                send[r - 512 : r - 256, :] = total


def bricks_of(cells, scale, stats, expo, images, weights):
    positions, width, voxels = weights.shape
    half = pl.BlockSpec((512, voxels), lambda i: (0, 0))
    return pl.pallas_call(
        bricks_kernel,
        grid=(VALUES // WIDE,),
        in_specs=[
            pl.BlockSpec(
                (WIDE // LANES * REFS,), lambda i: (i,), memory_space=pltpu.SMEM
            ),
            pl.BlockSpec((8, LANES), lambda i: (0, 0)),
            *[pl.BlockSpec((16, LANES), lambda i: (0, 0))] * 4,
            pl.BlockSpec((REFS, IMAGES), lambda i: (0, 0)),
            pl.BlockSpec((IMAGES, WIDE), lambda i: (0, i)),
            pl.BlockSpec((positions, width, voxels), lambda i: (0, 0, 0)),
        ],
        out_specs=[half, half, pl.BlockSpec((8, LANES), lambda i: (0, 0))],
        out_shape=[
            jax.ShapeDtypeStruct((512, voxels), F32),
            jax.ShapeDtypeStruct((512, voxels), F32),
            jax.ShapeDtypeStruct((8, LANES), F32),
        ],
        scratch_shapes=[
            pltpu.VMEM((REFS, IMAGES), BF16),
            pltpu.VMEM((WIDE // LANES * REFS, LANES), F32),
        ]
        + [pltpu.VMEM((CELLS, LANES), F32)] * SUMS,
        compiler_params=pltpu.CompilerParams(vmem_limit_bytes=VMEM),
        name="bricks",
    )(cells, scale, *stats, expo, images, weights)


def brick_share(keep, send):
    voxels = keep.shape[1]
    x = keep + moved(send, ("core",), lambda c: (c + 1,))
    x = x.reshape(16, -1, voxels).astype(BF16)
    x = jnp.sum(lax.all_to_all(x, ("y", "xl", "xh"), 0, 0).astype(F32), axis=0)
    x = x.reshape(2, -1, voxels)
    x = x[0] + moved(x[1], ("z",), lambda z: (z ^ 4,))
    x = x.reshape(4, -1, voxels)
    return x[0] + sum([moved(x[k], ("z",), lambda z: (z ^ k,)) for k in (1, 2, 3)])


def body(images, img_scale, references, pattern, tile_owner, tile_brick, tile_block, weights):
    cut = 32
    at = {a: lax.axis_index(a) for a in AXES}
    owned = tile_owner.reshape(-1)
    codes = jnp.concatenate([owned, (tile_brick * 8 + tile_block).reshape(-1)])
    parts, code = gathered_references(references, codes, cut)

    code = code[..., : owned.size] * 128 + code[..., owned.size :]
    code = code.reshape(REFS, -1).T.reshape(-1)
    block, row = code % 8, code // 8 % 4
    core, xh = code // 32 % 2, code // 64 % 2
    z, xl, y = code // 128 % 8, code // 1024 % 2, code // 2048
    away = ((jnp.bitwise_xor(core, at["core"]) * 4 + y) * 2 + xl) * 2 + xh
    away = away * 8 + jnp.bitwise_xor(z, at["z"])
    cells = block * (CELLS // 8) + away * 4 + row

    me = jnp.stack([at["y"], at["xl"]]).astype(I32)
    expo, stats = scores_of(me, images, img_scale[:, None], pattern, parts, cut)
    others = [
        moved(stats, ORI, lambda h, c: (h + dh, c + dc)) for dh, dc in ((0, 1), (1, 0), (1, 1))
    ]
    scale = img_scale.reshape(8, LANES)
    keep, send, evidence = bricks_of(cells, scale, (stats, *others), expo, images, weights)
    return brick_share(keep, send), evidence.reshape(-1)


def solution(mesh):
    cut_mesh = Mesh(mesh.devices.reshape(*AXES.values()), tuple(AXES))
    placed = (
        P(IMG, None),
        P(IMG),
        P(ORI, IMG),
        P(IMG, ORI),
        P(ORI, IMG, None),
        P(ORI, IMG),
        P(ORI, IMG),
        P(),
    )
    return jax.shard_map(
        body,
        mesh=cut_mesh,
        in_specs=placed,
        out_specs=(P(IMG + ORI, None), P(IMG)),
        check_vma=False,
    )
```

```python
import functools
import math

import jax
import jax.numpy as jnp
from jax import lax
from jax.experimental import pallas as pl
from jax.experimental.pallas import tpu as pltpu
from jax.sharding import Mesh
from jax.sharding import PartitionSpec as P

BF16, F32, I32 = jnp.bfloat16, jnp.float32, jnp.int32
AXES = {"y": 4, "xl": 2, "z": 8, "xh": 2, "core": 2}
IMG, ORI = ("y", "xl", "z"), ("xh", "core")
REFS, VALUES, IMAGES = 512, 4096, 1024
SHARE = 64
CELLS = 8192
LANES = 128
VMEM = 58 * 2**20


def moved(x, axes, target):
    sizes = [AXES[a] for a in axes]
    pairs = []
    for i in range(math.prod(sizes)):
        at, k = [], i
        for n in reversed(sizes):
            at.insert(0, k % n)
            k //= n
        to = 0
        for n, c in zip(sizes, target(*at)):
            to = to * n + c % n
        pairs.append((i, to))
    return lax.ppermute(x, axes, pairs)


def spread(x, axes):
    n = math.prod(AXES[a] for a in axes)
    return lax.all_to_all(jnp.broadcast_to(x[None], (n, *x.shape)), axes, 0, 0)


def gathered_references(references, codes, cut):
    share = references.T
    near = spread(share[:cut], ("y", "xl"))
    ended_z = lax.all_gather(near, "z", axis=0)
    more = jnp.pad(codes.astype(BF16)[None], ((0, 7), (0, 0)))
    own = spread(jnp.concatenate([share[cut:], more]), ("z",))
    codes, own = own[:, SHARE - cut], own[:, : SHARE - cut]
    other = moved(own, ("xl",), lambda xl: (xl + 1,))
    near = [own] + [moved(own, ("y",), lambda y: (y + d,)) for d in (1, 2, 3)]
    far = [other] + [moved(other, ("y",), lambda y: (y + d,)) for d in (1, 3)]
    far.insert(2, moved(near[2], ("xl",), lambda xl: (xl + 1,)))
    codes, _ = lax.optimization_barrier((codes, other))
    codes = spread(codes, ("y", "xl")).astype(I32)
    return [ended_z, *near, *far], codes


def eye():
    return lax.broadcasted_iota(I32, (LANES, LANES), 0) == lax.broadcasted_iota(
        I32, (LANES, LANES), 1
    )


def scores_kernel(
    cut, me, images, scale, pattern, by_z, a0, a1, a2, a3, b0, b1, b2, b3, expo, stats, refs, sems
):
    step = pl.program_id(0)
    rows = images.shape[0]

    @pl.when(step == 0)
    def _():
        copies = [(by_z.at[z], refs.at[:, z, pl.ds(0, cut)]) for z in range(8)]
        for i, part in enumerate((a0, a1, a2, a3, b0, b1, b2, b3)):
            y, xl = (me[0] + 4 - i % 4) % 4, (me[1] + i // 4) % 2
            copies.append((part, refs.at[y * 2 + xl, :, pl.ds(cut, SHARE - cut)]))
        for i, (a, b) in enumerate(copies):
            pltpu.make_async_copy(a, b, sems.at[i]).start()
        for i, (a, b) in enumerate(copies):
            pltpu.make_async_copy(a, b, sems.at[i]).wait()

    total = jnp.dot(
        images[...], refs[...].reshape(VALUES, REFS), preferred_element_type=F32
    )
    scores = total * scale[...] * (1.0 / math.sqrt(VALUES))
    group = lax.broadcasted_iota(I32, (rows, REFS), 1) // (REFS // 2)
    flags = pattern[...]
    active = jnp.where(group == 0, flags[:, 0:1], flags[:, 1:2]) > 0
    masked = jnp.where(active, scores, -1e30)
    peak = jnp.max(masked, axis=1, keepdims=True)
    value = jnp.where(active, jnp.exp(masked - peak), 0.0)
    mass = jnp.sum(value, axis=1, keepdims=True)
    expo[...] = value.T
    for j in range(rows // LANES):
        part = slice(j * LANES, (j + 1) * LANES)
        at = step * (rows // LANES) + j
        for k, column in enumerate((peak, mass)):
            stats[pl.ds(k * 8 + at, 1), :] = jnp.sum(
                jnp.where(eye(), column[part], 0.0), axis=0, keepdims=True
            )


def scores_of(me, images, scale, pattern, parts, cut, rows=256):
    return pl.pallas_call(
        functools.partial(scores_kernel, cut),
        grid=(IMAGES // rows,),
        in_specs=[
            pl.BlockSpec(memory_space=pltpu.SMEM),
            pl.BlockSpec((rows, VALUES), lambda i: (i, 0)),
            pl.BlockSpec((rows, 1), lambda i: (i, 0)),
            pl.BlockSpec((rows, 2), lambda i: (i, 0)),
        ]
        + [pl.BlockSpec(memory_space=pl.ANY)] * len(parts),
        out_specs=[
            pl.BlockSpec((REFS, rows), lambda i: (0, i)),
            pl.BlockSpec((16, LANES), lambda i: (0, 0)),
        ],
        out_shape=[
            jax.ShapeDtypeStruct((REFS, IMAGES), F32),
            jax.ShapeDtypeStruct((16, LANES), F32),
        ],
        scratch_shapes=[
            pltpu.VMEM((8, 8, SHARE, REFS), BF16),
            pltpu.SemaphoreType.DMA((16,)),
        ],
        compiler_params=pltpu.CompilerParams(vmem_limit_bytes=VMEM),
        name="scores",
    )(me, images, scale, pattern, *parts)


UNROLL = 128
SUMS = 8
WIDE = 1024


def bricks_kernel(
    cells, scale, s0, s1, s2, s3, expo, images, weights,
    keep, send, evidence, scaled, tiles, *sums,
):
    step = pl.program_id(0)

    @pl.when(step == 0)
    def _():
        pairs = [(s[0:8, :], s[8:16, :]) for s in (s0, s1, s2, s3)]
        peak = functools.reduce(jnp.maximum, [p for p, _ in pairs])
        mass = sum(m * jnp.exp(p - peak) for p, m in pairs)
        evidence[...] = peak + jnp.log(mass)
        factor = jnp.exp(pairs[0][0] - peak) / mass * scale[...]
        for j in range(IMAGES // LANES):
            part = slice(j * LANES, (j + 1) * LANES)
            scaled[:, part] = (expo[:, part] * factor[j : j + 1, :]).astype(BF16)

        def clear(i, _):
            for c in sums:
                c[pl.ds(i * 256, 256), :] = jnp.zeros((256, LANES), F32)
            return 0

        lax.fori_loop(0, CELLS // 256, clear, 0)

    for n in range(0, WIDE, 256):
        block = jnp.dot(scaled[...], images[:, n : n + 256], preferred_element_type=F32)
        for k in range(2):
            at = (n // LANES + k) * REFS
            tiles[at : at + REFS, :] = block[:, k * LANES : (k + 1) * LANES]

    count = tiles.shape[0]

    def add(i, _):
        for u in range(UNROLL):
            row = i * UNROLL + u
            cell = pl.ds(cells[row], 1)
            c = sums[u % SUMS]
            c[cell, :] = c[cell, :] + tiles[pl.ds(row, 1), :]
        return 0

    lax.fori_loop(0, count // UNROLL, add, 0)

    @pl.when(step == pl.num_programs(0) - 1)
    def _():
        for r, out in ((0, keep), (512, send)):
            total = jnp.zeros((512, weights.shape[2]), F32)
            for p in range(8):
                part = pl.ds(p * 1024 + r, 512)
                cell = functools.reduce(jnp.add, [c[part, :] for c in sums])
                high = cell.astype(BF16)
                low = (cell - high.astype(F32)).astype(BF16)
                w = weights[p]
                total += jnp.dot(
                    jnp.concatenate([high, low], axis=1),
                    jnp.concatenate([w, w], axis=0),
                    preferred_element_type=F32,
                )
            out[...] = total


def bricks_of(cells, scale, stats, expo, images, weights):
    positions, width, voxels = weights.shape
    half = pl.BlockSpec((512, voxels), lambda i: (0, 0))
    return pl.pallas_call(
        bricks_kernel,
        grid=(VALUES // WIDE,),
        in_specs=[
            pl.BlockSpec(
                (WIDE // LANES * REFS,), lambda i: (i,), memory_space=pltpu.SMEM
            ),
            pl.BlockSpec((8, LANES), lambda i: (0, 0)),
            *[pl.BlockSpec((16, LANES), lambda i: (0, 0))] * 4,
            pl.BlockSpec((REFS, IMAGES), lambda i: (0, 0)),
            pl.BlockSpec((IMAGES, WIDE), lambda i: (0, i)),
            pl.BlockSpec((positions, width, voxels), lambda i: (0, 0, 0)),
        ],
        out_specs=[half, half, pl.BlockSpec((8, LANES), lambda i: (0, 0))],
        out_shape=[
            jax.ShapeDtypeStruct((512, voxels), F32),
            jax.ShapeDtypeStruct((512, voxels), F32),
            jax.ShapeDtypeStruct((8, LANES), F32),
        ],
        scratch_shapes=[
            pltpu.VMEM((REFS, IMAGES), BF16),
            pltpu.VMEM((WIDE // LANES * REFS, LANES), F32),
        ]
        + [pltpu.VMEM((CELLS, LANES), F32)] * SUMS,
        compiler_params=pltpu.CompilerParams(vmem_limit_bytes=VMEM),
        name="bricks",
    )(cells, scale, *stats, expo, images, weights)


def brick_share(keep, send):
    voxels = keep.shape[1]
    x = keep + moved(send, ("core",), lambda c: (c + 1,))
    x = x.reshape(16, -1, voxels).astype(BF16)
    x = jnp.sum(lax.all_to_all(x, ("y", "xl", "xh"), 0, 0).astype(F32), axis=0)
    x = x.reshape(2, -1, voxels)
    x = x[0] + moved(x[1], ("z",), lambda z: (z ^ 4,))
    x = x.reshape(4, -1, voxels)
    return x[0] + sum([moved(x[k], ("z",), lambda z: (z ^ k,)) for k in (1, 2, 3)])


def body(images, img_scale, references, pattern, tile_owner, tile_brick, tile_block, weights):
    cut = 32
    at = {a: lax.axis_index(a) for a in AXES}
    owned = tile_owner.reshape(-1)
    codes = jnp.concatenate([owned, (tile_brick * 8 + tile_block).reshape(-1)])
    parts, code = gathered_references(references, codes, cut)

    code = code[..., : owned.size] * 128 + code[..., owned.size :]
    code = code.reshape(REFS, -1).T.reshape(-1)
    block, row = code % 8, code // 8 % 4
    core, xh = code // 32 % 2, code // 64 % 2
    z, xl, y = code // 128 % 8, code // 1024 % 2, code // 2048
    away = ((jnp.bitwise_xor(core, at["core"]) * 4 + y) * 2 + xl) * 2 + xh
    away = away * 8 + jnp.bitwise_xor(z, at["z"])
    cells = block * (CELLS // 8) + away * 4 + row

    me = jnp.stack([at["y"], at["xl"]]).astype(I32)
    expo, stats = scores_of(me, images, img_scale[:, None], pattern, parts, cut)
    others = [
        moved(stats, ORI, lambda h, c: (h + dh, c + dc)) for dh, dc in ((0, 1), (1, 0), (1, 1))
    ]
    scale = img_scale.reshape(8, LANES)
    keep, send, evidence = bricks_of(cells, scale, (stats, *others), expo, images, weights)
    return brick_share(keep, send), evidence.reshape(-1)


def solution(mesh):
    cut_mesh = Mesh(mesh.devices.reshape(*AXES.values()), tuple(AXES))
    placed = (
        P(IMG, None),
        P(IMG),
        P(ORI, IMG),
        P(IMG, ORI),
        P(ORI, IMG, None),
        P(ORI, IMG),
        P(ORI, IMG),
        P(),
    )
    return jax.shard_map(
        body,
        mesh=cut_mesh,
        in_specs=placed,
        out_specs=(P(IMG + ORI, None), P(IMG)),
        check_vma=False,
    )
```

```python
import functools
import math

import jax
import jax.numpy as jnp
from jax import lax
from jax.experimental import pallas as pl
from jax.experimental.pallas import tpu as pltpu
from jax.sharding import Mesh
from jax.sharding import PartitionSpec as P

BF16, F32, I32 = jnp.bfloat16, jnp.float32, jnp.int32
AXES = {"y": 4, "xl": 2, "z": 8, "xh": 2, "core": 2}
IMG, ORI = ("y", "xl", "z"), ("xh", "core")
REFS, VALUES, IMAGES = 512, 4096, 1024
SHARE = 64
CELLS = 8192
LANES = 128
VMEM = 58 * 2**20


def moved(x, axes, target):
    sizes = [AXES[a] for a in axes]
    pairs = []
    for i in range(math.prod(sizes)):
        at, k = [], i
        for n in reversed(sizes):
            at.insert(0, k % n)
            k //= n
        to = 0
        for n, c in zip(sizes, target(*at)):
            to = to * n + c % n
        pairs.append((i, to))
    return lax.ppermute(x, axes, pairs)


def spread(x, axes):
    n = math.prod(AXES[a] for a in axes)
    return lax.all_to_all(jnp.broadcast_to(x[None], (n, *x.shape)), axes, 0, 0)


def gathered_references(references, codes, cut):
    share = references.T
    near = spread(share[:cut], ("y", "xl"))
    ended_z = lax.all_gather(near, "z", axis=0)
    more = jnp.pad(codes.astype(BF16)[None], ((0, 7), (0, 0)))
    own = spread(jnp.concatenate([share[cut:], more]), ("z",))
    codes, own = own[:, SHARE - cut], own[:, : SHARE - cut]
    other = moved(own, ("xl",), lambda xl: (xl + 1,))
    near = [own] + [moved(own, ("y",), lambda y: (y + d,)) for d in (1, 2, 3)]
    far = [other] + [moved(other, ("y",), lambda y: (y + d,)) for d in (1, 3)]
    far.insert(2, moved(near[2], ("xl",), lambda xl: (xl + 1,)))
    codes, _ = lax.optimization_barrier((codes, other))
    codes = spread(codes, ("y", "xl")).astype(I32)
    return [ended_z, *near, *far], codes


def eye():
    return lax.broadcasted_iota(I32, (LANES, LANES), 0) == lax.broadcasted_iota(
        I32, (LANES, LANES), 1
    )


def scores_kernel(
    cut, me, images, scale, pattern, by_z, a0, a1, a2, a3, b0, b1, b2, b3, expo, stats, refs, sems
):
    step = pl.program_id(0)
    rows = images.shape[0]

    @pl.when(step == 0)
    def _():
        copies = [(by_z.at[z], refs.at[:, z, pl.ds(0, cut)]) for z in range(8)]
        for i, part in enumerate((a0, a1, a2, a3, b0, b1, b2, b3)):
            y, xl = (me[0] + 4 - i % 4) % 4, (me[1] + i // 4) % 2
            copies.append((part, refs.at[y * 2 + xl, :, pl.ds(cut, SHARE - cut)]))
        for i, (a, b) in enumerate(copies):
            pltpu.make_async_copy(a, b, sems.at[i]).start()
        for i, (a, b) in enumerate(copies):
            pltpu.make_async_copy(a, b, sems.at[i]).wait()

    total = jnp.dot(
        images[...], refs[...].reshape(VALUES, REFS), preferred_element_type=F32
    )
    scores = total * scale[...] * (1.0 / math.sqrt(VALUES))
    group = lax.broadcasted_iota(I32, (rows, REFS), 1) // (REFS // 2)
    flags = pattern[...]
    active = jnp.where(group == 0, flags[:, 0:1], flags[:, 1:2]) > 0
    masked = jnp.where(active, scores, -1e30)
    peak = jnp.max(masked, axis=1, keepdims=True)
    value = jnp.where(active, jnp.exp(masked - peak), 0.0)
    mass = jnp.sum(value, axis=1, keepdims=True)
    expo[...] = value.T
    for j in range(rows // LANES):
        part = slice(j * LANES, (j + 1) * LANES)
        at = step * (rows // LANES) + j
        for k, column in enumerate((peak, mass)):
            stats[pl.ds(k * 8 + at, 1), :] = jnp.sum(
                jnp.where(eye(), column[part], 0.0), axis=0, keepdims=True
            )


def scores_of(me, images, scale, pattern, parts, cut, rows=256):
    return pl.pallas_call(
        functools.partial(scores_kernel, cut),
        grid=(IMAGES // rows,),
        in_specs=[
            pl.BlockSpec(memory_space=pltpu.SMEM),
            pl.BlockSpec((rows, VALUES), lambda i: (i, 0)),
            pl.BlockSpec((rows, 1), lambda i: (i, 0)),
            pl.BlockSpec((rows, 2), lambda i: (i, 0)),
        ]
        + [pl.BlockSpec(memory_space=pl.ANY)] * len(parts),
        out_specs=[
            pl.BlockSpec((REFS, rows), lambda i: (0, i)),
            pl.BlockSpec((16, LANES), lambda i: (0, 0)),
        ],
        out_shape=[
            jax.ShapeDtypeStruct((REFS, IMAGES), F32),
            jax.ShapeDtypeStruct((16, LANES), F32),
        ],
        scratch_shapes=[
            pltpu.VMEM((8, 8, SHARE, REFS), BF16),
            pltpu.SemaphoreType.DMA((16,)),
        ],
        compiler_params=pltpu.CompilerParams(vmem_limit_bytes=VMEM),
        name="scores",
    )(me, images, scale, pattern, *parts)


UNROLL = 128
SUMS = 8
WIDE = 2048


def bricks_kernel(
    cells, scale, s0, s1, s2, s3, expo, images, weights,
    keep, send, evidence, scaled, tiles, *sums,
):
    step = pl.program_id(0)

    @pl.when(step == 0)
    def _():
        pairs = [(s[0:8, :], s[8:16, :]) for s in (s0, s1, s2, s3)]
        peak = functools.reduce(jnp.maximum, [p for p, _ in pairs])
        mass = sum(m * jnp.exp(p - peak) for p, m in pairs)
        evidence[...] = peak + jnp.log(mass)
        factor = jnp.exp(pairs[0][0] - peak) / mass * scale[...]
        for j in range(IMAGES // LANES):
            part = slice(j * LANES, (j + 1) * LANES)
            scaled[:, part] = (expo[:, part] * factor[j : j + 1, :]).astype(BF16)

        def clear(i, _):
            for c in sums:
                c[pl.ds(i * 256, 256), :] = jnp.zeros((256, LANES), F32)
            return 0

        lax.fori_loop(0, CELLS // 256, clear, 0)

    for n in range(0, WIDE, 256):
        block = jnp.dot(scaled[...], images[:, n : n + 256], preferred_element_type=F32)
        for k in range(2):
            at = (n // LANES + k) * REFS
            tiles[at : at + REFS, :] = block[:, k * LANES : (k + 1) * LANES]

    count = tiles.shape[0]

    def add(i, _):
        for u in range(UNROLL):
            row = i * UNROLL + u
            cell = pl.ds(cells[row], 1)
            c = sums[u % SUMS]
            c[cell, :] = c[cell, :] + tiles[pl.ds(row, 1), :]
        return 0

    lax.fori_loop(0, count // UNROLL, add, 0)

    @pl.when(step == pl.num_programs(0) - 1)
    def _():
        for r, out in ((0, keep), (512, send)):
            total = jnp.zeros((512, weights.shape[2]), F32)
            for p in range(8):
                part = pl.ds(p * 1024 + r, 512)
                cell = functools.reduce(jnp.add, [c[part, :] for c in sums])
                high = cell.astype(BF16)
                low = (cell - high.astype(F32)).astype(BF16)
                w = weights[p]
                total += jnp.dot(
                    jnp.concatenate([high, low], axis=1),
                    jnp.concatenate([w, w], axis=0),
                    preferred_element_type=F32,
                )
            out[...] = total


def bricks_of(cells, scale, stats, expo, images, weights):
    positions, width, voxels = weights.shape
    half = pl.BlockSpec((512, voxels), lambda i: (0, 0))
    return pl.pallas_call(
        bricks_kernel,
        grid=(VALUES // WIDE,),
        in_specs=[
            pl.BlockSpec(
                (WIDE // LANES * REFS,), lambda i: (i,), memory_space=pltpu.SMEM
            ),
            pl.BlockSpec((8, LANES), lambda i: (0, 0)),
            *[pl.BlockSpec((16, LANES), lambda i: (0, 0))] * 4,
            pl.BlockSpec((REFS, IMAGES), lambda i: (0, 0)),
            pl.BlockSpec((IMAGES, WIDE), lambda i: (0, i)),
            pl.BlockSpec((positions, width, voxels), lambda i: (0, 0, 0)),
        ],
        out_specs=[half, half, pl.BlockSpec((8, LANES), lambda i: (0, 0))],
        out_shape=[
            jax.ShapeDtypeStruct((512, voxels), F32),
            jax.ShapeDtypeStruct((512, voxels), F32),
            jax.ShapeDtypeStruct((8, LANES), F32),
        ],
        scratch_shapes=[
            pltpu.VMEM((REFS, IMAGES), BF16),
            pltpu.VMEM((WIDE // LANES * REFS, LANES), F32),
        ]
        + [pltpu.VMEM((CELLS, LANES), F32)] * SUMS,
        compiler_params=pltpu.CompilerParams(vmem_limit_bytes=VMEM),
        name="bricks",
    )(cells, scale, *stats, expo, images, weights)


def brick_share(keep, send):
    voxels = keep.shape[1]
    x = keep + moved(send, ("core",), lambda c: (c + 1,))
    x = x.reshape(16, -1, voxels).astype(BF16)
    x = jnp.sum(lax.all_to_all(x, ("y", "xl", "xh"), 0, 0).astype(F32), axis=0)
    x = x.reshape(2, -1, voxels)
    x = x[0] + moved(x[1], ("z",), lambda z: (z ^ 4,))
    x = x.reshape(4, -1, voxels)
    return x[0] + sum([moved(x[k], ("z",), lambda z: (z ^ k,)) for k in (1, 2, 3)])


def body(images, img_scale, references, pattern, tile_owner, tile_brick, tile_block, weights):
    cut = 32
    at = {a: lax.axis_index(a) for a in AXES}
    owned = tile_owner.reshape(-1)
    codes = jnp.concatenate([owned, (tile_brick * 8 + tile_block).reshape(-1)])
    parts, code = gathered_references(references, codes, cut)

    code = code[..., : owned.size] * 128 + code[..., owned.size :]
    code = code.reshape(REFS, -1).T.reshape(-1)
    block, row = code % 8, code // 8 % 4
    core, xh = code // 32 % 2, code // 64 % 2
    z, xl, y = code // 128 % 8, code // 1024 % 2, code // 2048
    away = ((jnp.bitwise_xor(core, at["core"]) * 4 + y) * 2 + xl) * 2 + xh
    away = away * 8 + jnp.bitwise_xor(z, at["z"])
    cells = block * (CELLS // 8) + away * 4 + row

    me = jnp.stack([at["y"], at["xl"]]).astype(I32)
    expo, stats = scores_of(me, images, img_scale[:, None], pattern, parts, cut)
    others = [
        moved(stats, ORI, lambda h, c: (h + dh, c + dc)) for dh, dc in ((0, 1), (1, 0), (1, 1))
    ]
    scale = img_scale.reshape(8, LANES)
    keep, send, evidence = bricks_of(cells, scale, (stats, *others), expo, images, weights)
    return brick_share(keep, send), evidence.reshape(-1)


def solution(mesh):
    cut_mesh = Mesh(mesh.devices.reshape(*AXES.values()), tuple(AXES))
    placed = (
        P(IMG, None),
        P(IMG),
        P(ORI, IMG),
        P(IMG, ORI),
        P(ORI, IMG, None),
        P(ORI, IMG),
        P(ORI, IMG),
        P(),
    )
    return jax.shard_map(
        body,
        mesh=cut_mesh,
        in_specs=placed,
        out_specs=(P(IMG + ORI, None), P(IMG)),
        check_vma=False,
    )
```
